512 devices in a mesh: op: 16 (over x, z_lo, core), sec: 32 (over y, z_hi).
Axes of the slice: x: 4, y: 8, z: 8 (z_hi: 4, z_lo: 2; z = z_hi * 2 + z_lo), core: 2. Of those that a mesh axis runs over, the one named last changes fastest.
Arguments:
- psi: float32 [64, 128, 128], P('sec', 'op'), may hold values from -6 to 6
- left_env: float32 [256, 64, 128, 128], P('op', 'sec'), may hold values from -0.078125 to 0.078125
- right_env: float32 [256, 64, 128, 128], P('op', 'sec'), may hold values from -0.5 to 0.5
- coupling: int32 [64, 256], P('sec', 'op'), may hold values from 0 to 63
- assign: int32 [64], replicated, may hold values from 0 to 63, each once
- sizes: int32 [64], replicated, may hold values from 1 to 128, 6144 in all
Outputs:
- sigma_first: float32 [64, 128, 128], P('sec', 'op')
- next_vector: float32 [64, 128, 128], P('sec', 'op')
- sigma_next: float32 [64, 128, 128], P('sec', 'op')
The draws below stay inside these ranges and needn't reach their ends.
Inputs may be any that keep to these rules, and one draw needn't show every extreme that they name: `assign`: each slot holds a different sector. `sizes`: sector dimensions sum to 64 * 128 * 3 // 4, the largest is exactly 128.
All inputs are finite; a program needn't handle non-finite values.
Results may differ from the reference program's by a relative error of at most 0.00011.
Values sent between devices are 32-bit elements; how exact they have to be, the bound alone decides.
No kernel may reach another device: no remote copies, remote signals or barrier semaphores. Data moves between devices by JAX's collectives and lax.ppermute only.
A program may use at most 64 MiB of HBM per device.

```python
import math
import jax
import jax.numpy as jnp
import numpy as np
from jax import lax

B = 128
SECTORS = 64
TERMS = 256


def place_ends(result, key, low, top_value):
    extent = result.shape
    place = [jax.random.randint(jax.random.fold_in(key, axis), (), 0, extent[axis]) for axis in range(len(extent))]
    result = result.at[tuple(place)].set(low)
    longest = extent.index(max(extent))
    place[longest] = (place[longest] + 1) % extent[longest]
    return result.at[tuple(place)].set(top_value)


def level_of(key, dims, split, smallest, top_value):
    def one(dim, blocks):
        heights = jax.random.uniform(jax.random.fold_in(jax.random.fold_in(key, 6), dim), (blocks,), jnp.float32, smallest / len(split), top_value / len(split))
        return jnp.repeat(jnp.exp(heights), dims[dim] // blocks).reshape((-1,) + (1,) * (len(dims) - dim - 1))

    loudness = one(*split[0])
    for cut in split[1:]:
        loudness = loudness * one(*cut)
    return loudness


def length_profile(amount, total, limit, skew):
    portions = [(1 << 20) // math.isqrt(grade ** skew) + 1 for grade in range(2, amount + 1)]
    spare, given = total - limit - (amount - 1), [1] * (amount - 1)
    while spare > 0:
        free = [i for i in range(amount - 1) if given[i] < limit]
        pool, left = sum([portions[i] for i in free]), spare
        for i in free:
            addition = min(limit - given[i], max(1, left * portions[i] // pool), spare)
            given[i] = given[i] + addition
            spare = spare - addition
    return np.array([limit] + given)


def uneven_parts(stream_key, amount, total, limit, slope):
    if amount == 2:
        one = jax.random.randint(stream_key, (), max(1, total - limit), min(limit, total - 1) + 1)
        return jnp.stack([one, total - one])
    tallies = jnp.asarray(length_profile(amount, total, limit, slope), jnp.int32)
    twos = (amount - 1) // 2
    giver, sink = tallies[1:1 + 2 * twos:2], tallies[2:2 + 2 * twos:2]
    slack = jnp.minimum(giver - 1, limit - sink)
    shifted = jax.random.randint(jax.random.fold_in(stream_key, 1), (twos,), 0, 1 << 20) % (slack + 1)
    tallies = tallies.at[1:1 + 2 * twos:2].set(giver - shifted).at[2:2 + 2 * twos:2].set(sink + shifted)
    return tallies[jax.random.permutation(jax.random.fold_in(stream_key, 2), amount)]


def noise(key, dims, scale, most, shards=(), kind=jnp.bfloat16):
    entries = jax.random.normal(key, dims, jnp.float32) * scale
    if len(shards) > 0:
        entries = level_of(key, dims, shards, -0.22, 0.18) * entries
    return jnp.clip(entries, min=-most, max=most).astype(kind)


def setup_inputs(seed: int = 0) -> dict:
    key_list = jax.random.split(jax.random.key(seed), 7)
    return {
        "psi": noise(key_list[0], (SECTORS, B, B), 1.0, 6.0, ((0, 32), (1, 16)), jnp.float32),
        "left_env": noise(key_list[1], (TERMS, SECTORS, B, B), ((B * TERMS) ** -0.5), 0.078125, ((0, 16), (1, 32)), jnp.float32),
        "right_env": noise(key_list[2], (TERMS, SECTORS, B, B), B ** -0.5, 0.5, ((0, 16), (1, 32)), jnp.float32),
        "coupling": place_ends(jax.random.randint(key_list[3], (SECTORS, TERMS), 0, SECTORS), jax.random.fold_in(key_list[3], 1), 0, SECTORS - 1).astype(jnp.int32),
        "assign": jax.random.permutation(key_list[4], SECTORS).astype(jnp.int32),
        "sizes": uneven_parts(key_list[5], SECTORS, SECTORS * B * 3 // 4, B, 2).astype(jnp.int32),
    }


def reference(psi, left_env, right_env, coupling, assign, sizes):
    sectors = assign.shape[0]
    width = psi.shape[1]
    labels = jnp.arange(sectors, dtype=jnp.int32)
    match = (assign[:, None] == labels[None, :]).astype(jnp.int32)
    slot_of = lax.optimization_barrier(jnp.sum(match * labels[:, None], axis=0))
    size_of = lax.optimization_barrier(jnp.sum(match * sizes[None, :], axis=1))
    cells = jnp.arange(width, dtype=jnp.int32)
    inside = (cells[None, :] < size_of[:, None]).astype(jnp.float32)
    mask = inside[:, :, None] * inside[:, None, :]
    source = slot_of[coupling]

    def apply(field):

        def one(slot):
            picked = field[source[slot]]
            lefts = left_env[:, slot]
            rights = right_env[:, slot]
            inner = jnp.einsum('kij,kjl->kil', lefts, picked, precision=lax.Precision.HIGHEST)
            return jnp.einsum('kil,kml->im', inner, rights, precision=lax.Precision.HIGHEST)
        return lax.map(one, jnp.arange(sectors, dtype=jnp.int32)) * mask
    start = psi * mask
    sigma_first = apply(start)
    theta = jnp.sum(start * sigma_first) / jnp.sum(start * start)
    resid = sigma_first - theta * start
    next_vector = resid / jnp.sqrt(jnp.sum(resid * resid) + 1e-06)
    sigma_next = apply(next_vector)
    return (sigma_first, next_vector, sigma_next)
```

```python
import itertools

import jax
import jax.numpy as jnp
from jax import lax
from jax.experimental import pallas as pl
from jax.experimental.pallas import tpu as pltpu
from jax.sharding import PartitionSpec as P

AXES = ("op", "sec")
F32 = jnp.float32
BF16 = jnp.bfloat16
SLOTS, ROWS, WIDTH, LOCAL_TERMS = 2, 8, 128, 16
SECTORS = 64
OPS, SECS = 16, 32
CHUNKS = 512


PLACES = list(itertools.product(range(4), range(2), range(2), range(8), range(4)))


def number(x, zl, core, y, zh):
    return ((((x * 2 + zl) * 2 + core) * 8) + y) * 4 + zh


def groups(key, order):
    found = {}
    for place in PLACES:
        found.setdefault(key(*place), []).append((order(*place), number(*place)))
    return [[device for _, device in sorted(members)] for members in found.values()]


def cube(x, zl, core, y, zh):
    z = 2 * zh + zl
    return (x - core) % 4 // 2, (y - core) % 8 // 2, (z - core) % 8 // 2, core


SAME_SEC = groups(lambda x, zl, core, y, zh: (y, zh), lambda x, zl, core, y, zh: (x, zl, core))
FAR = groups(lambda x, zl, core, y, zh: (x % 2, y % 2, zl, core), lambda x, zl, core, y, zh: (x // 2, y // 2, zh))
NEAR = groups(cube, lambda x, zl, core, y, zh: (x % 2, y % 2, zl))
OTHER_CORE = [
    (number(x, zl, core, y, zh), number(x, zl, 1 - core, y, zh)) for x, zl, core, y, zh in PLACES
]
ROW_STEPS = [(x % 2) * 256 + zl * 64 + (x // 2) * 32 for x in range(4) for zl in range(2)]


def exchange(parts, members):
    return lax.all_to_all(parts, AXES, 0, 0, axis_index_groups=members)


VMEM = pl.BlockSpec(memory_space=pltpu.VMEM)
SMEM = pl.BlockSpec(memory_space=pltpu.SMEM)


def call(body, outs, out_specs, in_specs, scratch=(), flops=0, moved=1 << 20):
    return pl.pallas_call(
        body,
        out_shape=outs,
        in_specs=in_specs,
        out_specs=out_specs,
        scratch_shapes=list(scratch),
        compiler_params=pltpu.CompilerParams(vmem_limit_bytes=40 << 20),
        cost_estimate=pl.CostEstimate(flops=flops, bytes_accessed=moved, transcendentals=0),
    )


def shape(*dims, dtype=F32):
    return jax.ShapeDtypeStruct(dims, dtype)


def row_mask(size, first_row):
    rows = first_row + lax.broadcasted_iota(jnp.int32, (ROWS, WIDTH), 0)
    cols = lax.broadcasted_iota(jnp.int32, (ROWS, WIDTH), 1)
    return (rows < size) & (cols < size)


def begin(place, psi, coupling, assign, sizes, start, copies, base, local_size, slot_of):
    for p in range(SECTORS):
        slot_of[assign[p]] = p
    for t in range(SLOTS):
        for k in range(LOCAL_TERMS):
            p = slot_of[coupling[t, k]]
            y = p // 8
            base[t, k] = (y % 2) * 128 + (y // 2) * 8 + p % 8
        size = sizes[assign[place[1] * SLOTS + t]]
        local_size[t] = size
        block = jnp.where(row_mask(size, place[0] * ROWS), psi[t], 0.0)
        start[t] = block
        for i in range(SECS):
            copies[i, t] = block


def halves(values):
    high = values.astype(BF16)
    return high, (values - high.astype(F32)).astype(BF16)


def split_envs(place, left, right, lefts, rights):
    core = place[0] % 2
    row = lax.broadcasted_iota(jnp.int32, (WIDTH, WIDTH), 0)
    col = lax.broadcasted_iota(jnp.int32, (WIDTH, WIDTH), 1)
    other = (row // 8 % 2 != core).astype(jnp.int32)
    order = (col == other * 64 + row // 16 * 8 + row % 8).astype(F32).astype(BF16)
    for k in range(LOCAL_TERMS):
        for t in range(SLOTS):
            high, low = halves(left[k, t])
            both = jnp.concatenate([high, low], axis=0)
            moved = lax.dot_general(both, order, (((1,), (0,)), ((), ())), preferred_element_type=F32).astype(BF16)
            lefts[k, t, :, :WIDTH] = moved[:WIDTH]
            lefts[k, t, :, WIDTH:] = moved[WIDTH:]
            high, low = halves(right[k, t].T)
            rights[k, t, :, :WIDTH] = high
            rights[k, t, :, WIDTH:] = low


def matmul(a, b):
    return lax.dot_general(a, b, (((1,), (0,)), ((), ())), preferred_element_type=F32)


def products(block_of, base, lefts, rights, store):
    for t in range(SLOTS):
        total = jnp.zeros((WIDTH, 2 * WIDTH), F32)
        for k in range(LOCAL_TERMS):
            high, low = halves(block_of(base[t, k]))
            pair = jnp.concatenate([high, low], axis=1)
            inner = matmul(lefts[k, t], jnp.concatenate([pair, pair], axis=0))
            high, low = halves(inner[:, :WIDTH] + inner[:, WIDTH:])
            rows = rights[k, t]
            total = total + matmul(
                jnp.concatenate([high, low], axis=1), jnp.concatenate([rows, rows], axis=0)
            )
        result = total[:, :WIDTH] + total[:, WIDTH:]
        for i in range(OPS):
            store(i, t, result[i * ROWS : (i + 1) * ROWS])


def gathered_block(mine, other, first):
    return jnp.concatenate(
        [mine[first + step] for step in ROW_STEPS] + [other[first + step] for step in ROW_STEPS], axis=0
    )


def apply_first(base, mine, other, lefts, rights, out):
    def store(i, t, rows):
        out[i, t] = rows

    products(lambda first: gathered_block(mine, other, first), base, lefts, rights, store)


def finish_first(place, local_size, parts, sigma, copies):
    for t in range(SLOTS):
        total = parts[0, t]
        for i in range(1, OPS):
            total = total + parts[i, t]
        total = jnp.where(row_mask(local_size[t], place[0] * ROWS), total, 0.0)
        sigma[t] = total
        for i in range(SECS):
            copies[i, t] = total


def scan(arrays, step, parts):
    lanes = 4

    def body(i, sums):
        sums = list(sums)
        for u in range(8):
            terms = step(*[a[i * 8 + u] for a in arrays])
            for n in range(parts):
                sums[n * lanes + u % lanes] = sums[n * lanes + u % lanes] + terms[n]
        return tuple(sums)

    zero = jnp.zeros((ROWS, WIDTH), F32)
    sums = lax.fori_loop(0, CHUNKS // 8, body, (zero,) * (parts * lanes))
    return [sum(sums[n * lanes : (n + 1) * lanes]) for n in range(parts)]


def whole_sum(values):
    return jnp.sum(jnp.sum(values, axis=1, keepdims=True), axis=0, keepdims=True)


def apply_next(
    base, start_mine, start_other, mine, other, lefts, rights, start, sigma, out, next_vector
):
    def moments(s, g):
        return s * g, s * s

    cross_a, square_a = scan((start_mine, mine), moments, 2)
    cross_b, square_b = scan((start_other, other), moments, 2)
    theta = whole_sum(cross_a + cross_b) / whole_sum(square_a + square_b)

    def residual(s, g):
        r = g - theta * s
        return (r * r,)

    (norm_a,) = scan((start_mine, mine), residual, 1)
    (norm_b,) = scan((start_other, other), residual, 1)
    scale = 1.0 / jnp.sqrt(whole_sum(norm_a + norm_b) + 1e-06)
    for t in range(SLOTS):
        next_vector[t] = (sigma[t] - theta * start[t]) * scale

    def block(first):
        return gathered_block(mine, other, first) - theta * gathered_block(start_mine, start_other, first)

    def store(i, t, rows):
        out[i, t] = rows * scale

    products(block, base, lefts, rights, store)


def finish_next(place, local_size, parts, sigma):
    for t in range(SLOTS):
        total = parts[0, t]
        for i in range(1, OPS):
            total = total + parts[i, t]
        sigma[t] = jnp.where(row_mask(local_size[t], place[0] * ROWS), total, 0.0)


def gather(copies):
    part = exchange(copies, FAR).reshape(1, CHUNKS // 8, ROWS, WIDTH)
    part = jnp.broadcast_to(part, (8, CHUNKS // 8, ROWS, WIDTH))
    mine = exchange(part, NEAR).reshape(CHUNKS, ROWS, WIDTH)
    return mine, lax.ppermute(mine, AXES, OTHER_CORE)


def on_device(psi, left_env, right_env, coupling, assign, sizes):
    place = jnp.stack([lax.axis_index("op"), lax.axis_index("sec")]).astype(jnp.int32)
    vec = shape(SLOTS, ROWS, WIDTH)
    copies_shape = shape(SECS, SLOTS, ROWS, WIDTH)
    parts_shape = shape(OPS, SLOTS, ROWS, WIDTH)
    env_shape = shape(LOCAL_TERMS, SLOTS, WIDTH, 2 * WIDTH, dtype=BF16)
    flops = 2 * 2 * 32 * 128 * 256 * 256

    start, copies, base, local_size = call(
        begin,
        (vec, copies_shape, shape(SLOTS, LOCAL_TERMS, dtype=jnp.int32), shape(SLOTS, dtype=jnp.int32)),
        (VMEM, VMEM, SMEM, SMEM),
        (SMEM, VMEM, SMEM, SMEM, SMEM),
        scratch=(pltpu.SMEM((SECTORS,), jnp.int32),),
    )(place, psi, coupling, assign, sizes)
    start_mine, start_other = gather(copies)
    lefts, rights = call(
        split_envs, (env_shape, env_shape), (VMEM, VMEM), (SMEM, VMEM, VMEM), flops=flops, moved=8 << 20
    )(place, left_env, right_env)
    parts = call(apply_first, parts_shape, VMEM, (SMEM,) + (VMEM,) * 4, flops=flops)(
        base, start_mine, start_other, lefts, rights
    )
    parts = exchange(parts, SAME_SEC)
    sigma_first, copies = call(finish_first, (vec, copies_shape), (VMEM, VMEM), (SMEM, SMEM, VMEM))(
        place, local_size, parts
    )
    mine, other = gather(copies)
    parts, next_vector = call(apply_next, (parts_shape, vec), (VMEM, VMEM), (SMEM,) + (VMEM,) * 8, flops=flops)(
        base, start_mine, start_other, mine, other, lefts, rights, start, sigma_first
    )
    parts = exchange(parts, SAME_SEC)
    sigma_next = call(finish_next, vec, VMEM, (SMEM, SMEM, VMEM))(place, local_size, parts)
    return sigma_first, next_vector, sigma_next


def solution(mesh):
    placed = (
        P("sec", "op", None),
        P("op", "sec", None, None),
        P("op", "sec", None, None),
        P("sec", "op"),
        P(),
        P(),
    )
    return jax.shard_map(
        on_device,
        mesh=mesh,
        in_specs=placed,
        out_specs=(P("sec", "op", None),) * 3,
        check_vma=False,
    )
```

```python
import itertools

import jax
import jax.numpy as jnp
from jax import lax
from jax.experimental import pallas as pl
from jax.experimental.pallas import tpu as pltpu
from jax.sharding import PartitionSpec as P

AXES = ("op", "sec")
F32 = jnp.float32
BF16 = jnp.bfloat16
SLOTS, ROWS, WIDTH, LOCAL_TERMS = 2, 8, 128, 16
SECTORS = 64
OPS, SECS = 16, 32
CHUNKS = 512


PLACES = list(itertools.product(range(4), range(2), range(2), range(8), range(4)))


def number(x, zl, core, y, zh):
    return ((((x * 2 + zl) * 2 + core) * 8) + y) * 4 + zh


def groups(key, order):
    found = {}
    for place in PLACES:
        found.setdefault(key(*place), []).append((order(*place), number(*place)))
    return [[device for _, device in sorted(members)] for members in found.values()]


def cube(x, zl, core, y, zh):
    z = 2 * zh + zl
    return (x - core) % 4 // 2, (y - core) % 8 // 2, (z - core) % 8 // 2, core


SAME_SEC = groups(lambda x, zl, core, y, zh: (y, zh), lambda x, zl, core, y, zh: (x, zl, core))
FAR = groups(lambda x, zl, core, y, zh: (x % 2, y % 2, zl, core), lambda x, zl, core, y, zh: (y // 2, zh, x // 2))
FAR_YZ = groups(lambda x, zl, core, y, zh: (x, y % 2, zl, core), lambda x, zl, core, y, zh: (y // 2, zh))
NEAR = groups(cube, lambda x, zl, core, y, zh: (x % 2, y % 2, zl))
OTHER_CORE = [
    (number(x, zl, core, y, zh), number(x, zl, 1 - core, y, zh)) for x, zl, core, y, zh in PLACES
]
ROW_STEPS = [(x % 2) * 256 + zl * 64 + (x // 2) * 2 for x in range(4) for zl in range(2)]


def exchange(parts, members):
    return lax.all_to_all(parts, AXES, 0, 0, axis_index_groups=members)


VMEM = pl.BlockSpec(memory_space=pltpu.VMEM)
SMEM = pl.BlockSpec(memory_space=pltpu.SMEM)
HBM = pl.BlockSpec(memory_space=pltpu.HBM)


def call(body, outs, out_specs, in_specs, scratch=(), flops=0, moved=1 << 20, aliases=None):
    return pl.pallas_call(
        body,
        out_shape=outs,
        in_specs=in_specs,
        out_specs=out_specs,
        scratch_shapes=list(scratch),
        input_output_aliases=aliases or {},
        compiler_params=pltpu.CompilerParams(vmem_limit_bytes=40 << 20),
        cost_estimate=pl.CostEstimate(flops=flops, bytes_accessed=moved, transcendentals=0),
    )


def shape(*dims, dtype=F32):
    return jax.ShapeDtypeStruct(dims, dtype)


def inside(size, first_row):
    rows = first_row + lax.broadcasted_iota(jnp.int32, (ROWS, WIDTH), 0)
    cols = lax.broadcasted_iota(jnp.int32, (ROWS, WIDTH), 1)
    return (rows < size) & (cols < size)


def fetch(pairs, done):
    copies = [pltpu.make_async_copy(source, target, done.at[i]) for i, (source, target) in enumerate(pairs)]
    for copy in copies:
        copy.start()
    for copy in copies:
        copy.wait()


def halves(values):
    high = values.astype(BF16)
    return high, (values - high.astype(F32)).astype(BF16)


def prepare(
    coupling_hbm, assign_hbm, sizes_hbm, left, right, base, size_of, masks, lefts, rights, coupling, assign, sizes, slot_of, done
):
    fetch([(coupling_hbm, coupling), (assign_hbm, assign), (sizes_hbm, sizes)], done)
    op = lax.axis_index("op")
    for p in range(SECTORS):
        sector = assign[p]
        slot_of[sector] = p
        size_of[p] = sizes[sector]
    for t in range(SLOTS):
        for k in range(LOCAL_TERMS):
            p = slot_of[coupling[t, k]]
            y = p // 8
            base[t, k] = (y % 2) * 128 + (y // 2) * 16 + p % 8 // 2 * 4 + p % 2
        size = size_of[lax.axis_index("sec") * SLOTS + t]
        for xh in range(2):
            masks[xh, t] = inside(size, (xh * 8 + op % 8) * ROWS).astype(F32)
    row = lax.broadcasted_iota(jnp.int32, (WIDTH, WIDTH), 0)
    col = lax.broadcasted_iota(jnp.int32, (WIDTH, WIDTH), 1)
    other = (row // 8 % 2 != op % 2).astype(jnp.int32)
    order = (col == other * 64 + row // 16 * 8 + row % 8).astype(F32).astype(BF16)
    for k in range(LOCAL_TERMS):
        for t in range(SLOTS):
            size = sizes[coupling[t, k]]
            high, low = halves(jnp.where(col < size, left[k, t], 0.0))
            moved = matmul(jnp.concatenate([high, low], axis=0), order).astype(BF16)
            lefts[k, t, :, :WIDTH] = moved[:WIDTH]
            lefts[k, t, :, WIDTH:] = moved[WIDTH:]
            high, low = halves(jnp.where(col < size, right[k, t], 0.0).T)
            rights[k, t, :, :WIDTH] = high
            rights[k, t, :, WIDTH:] = low


def matmul(a, b):
    return lax.dot_general(a, b, (((1,), (0,)), ((), ())), preferred_element_type=F32)


def products(block_of, base, lefts, rights, store, beside=None):
    results = []
    for t in range(SLOTS):
        total = jnp.zeros((WIDTH, 2 * WIDTH), F32)
        for k in range(LOCAL_TERMS):
            if beside is not None:
                beside(t * LOCAL_TERMS + k)
            high, low = halves(block_of(base[t, k]))
            pair = jnp.concatenate([high, low], axis=1)
            inner = matmul(lefts[k, t], jnp.concatenate([pair, pair], axis=0))
            high, low = halves(inner[:, :WIDTH] + inner[:, WIDTH:])
            rows = rights[k, t]
            total = total + matmul(
                jnp.concatenate([high, low], axis=1), jnp.concatenate([rows, rows], axis=0)
            )
        results.append(total[:, :WIDTH] + total[:, WIDTH:])
    for t in range(SLOTS):
        for i in range(OPS):
            store(i, t, results[t][i * ROWS : (i + 1) * ROWS])


def gathered_block(mine, other, first):
    return jnp.concatenate(
        [mine[first + step] for step in ROW_STEPS] + [other[first + step] for step in ROW_STEPS], axis=0
    )


def apply_first(base, mine, other, lefts, rights, out):
    def store(i, t, rows):
        for x in range(2):
            out[x * 8 + i % 8, i // 8, t] = rows

    products(lambda first: gathered_block(mine, other, first), base, lefts, rights, store)


def finish_first(masks, parts, sigma, copies):
    mine = lax.axis_index("op") // 8
    for xh in range(2):
        for t in range(SLOTS):
            total = parts[0, xh, t]
            for i in range(1, OPS):
                total = total + parts[i, xh, t]
            total = total * masks[xh, t]
            for i in range(OPS):
                copies[i, xh, t] = total
    for t in range(SLOTS):
        sigma[t] = copies[0, mine, t]


LANES = 4


def scan(step, sums):
    def body(i, sums):
        sums = list(sums)
        for u in range(16):
            for n, term in enumerate(step(i * 16 + u)):
                sums[n * LANES + u % LANES] = sums[n * LANES + u % LANES] + term
        return tuple(sums)

    zero = jnp.zeros((ROWS, WIDTH), F32)
    sums = lax.fori_loop(0, CHUNKS // 16, body, (zero,) * (sums * LANES))
    return [sum(sums[n : n + LANES]) for n in range(0, len(sums), LANES)]


def moments(size_of, start_mine, start_other, mine, masked_mine, masked_other, sums):
    core = lax.axis_index("op") % 2
    rows = lax.broadcasted_iota(jnp.int32, (ROWS, WIDTH), 0)
    cols = lax.broadcasted_iota(jnp.int32, (ROWS, WIDTH), 1)

    def body(i, sums):
        sums = list(sums)
        xl, yl, zl, yh = i // 16, i // 8 % 2, i // 4 % 2, i % 4
        for u in range(16):
            zh, xh, t = u // 4, u // 2 % 2, u % 2
            size = size_of[(yh * 2 + yl) * 8 + zh * 2 + t]
            pair = (xh * 4 + xl * 2 + zl) * 2
            here = i * 16 + u
            wide = cols < size
            m = jnp.where(wide & (rows < size - (pair + core) * ROWS), start_mine[here], 0.0)
            o = jnp.where(wide & (rows < size - (pair + 1 - core) * ROWS), start_other[here], 0.0)
            masked_mine[here] = m
            masked_other[here] = o
            lane = u % LANES
            sums[lane] = sums[lane] + m * mine[here]
            sums[LANES + lane] = sums[LANES + lane] + (m * m + o * o)
        return tuple(sums)

    totals = lax.fori_loop(0, CHUNKS // 16, body, (jnp.zeros((ROWS, WIDTH), F32),) * (2 * LANES))
    sums[0] = sum(totals[:LANES])
    sums[1] = sum(totals[LANES:])


def whole_sum(values):
    return jnp.sum(jnp.sum(values, axis=1, keepdims=True), axis=0, keepdims=True)


def apply_next(
    base, start_mine, start_other, mine, other, lefts, rights, psi, masks, sigma, sums, out, next_vector
):
    (cross,) = scan(lambda i: (start_other[i] * other[i],), 1)
    theta = whole_sum(cross + sums[0]) / whole_sum(sums[1])
    norms = [jnp.zeros((ROWS, WIDTH), F32)] * LANES

    def beside(n):
        each = CHUNKS // (SLOTS * LOCAL_TERMS)
        for i in range(n * each, (n + 1) * each):
            for s, g in ((start_mine, mine), (start_other, other)):
                r = g[i] - theta * s[i]
                norms[i % LANES] = norms[i % LANES] + r * r

    def block(first):
        return gathered_block(mine, other, first) - theta * gathered_block(start_mine, start_other, first)

    scale = []

    def store(i, t, rows):
        if not scale:
            scale.append(1.0 / jnp.sqrt(whole_sum(sum(norms)) + 1e-06))
        out[i, t] = rows * scale[0]

    products(block, base, lefts, rights, store, beside)
    xh = lax.axis_index("op") // 8
    for t in range(SLOTS):
        next_vector[t] = (sigma[t] - theta * (psi[t] * masks[xh, t])) * scale[0]


def finish_next(masks, parts, sigma):
    mine = lax.axis_index("op") // 8
    for t in range(SLOTS):
        total = parts[0, t]
        for i in range(1, OPS):
            total = total + parts[i, t]
        sigma[t] = total * masks[mine, t]


def gather(copies, far):
    part = exchange(copies, far).reshape(1, CHUNKS // 8, ROWS, WIDTH)
    part = jnp.broadcast_to(part, (8, CHUNKS // 8, ROWS, WIDTH))
    mine = exchange(part, NEAR).reshape(CHUNKS, ROWS, WIDTH)
    return mine, lax.ppermute(mine, AXES, OTHER_CORE)


def on_device(psi, left_env, right_env, coupling, assign, sizes):
    ints = jnp.int32
    vec = shape(SLOTS, ROWS, WIDTH)
    env_shape = shape(LOCAL_TERMS, SLOTS, WIDTH, 2 * WIDTH, dtype=BF16)
    flops = 2 * 2 * 32 * 128 * 256 * 256

    start_mine, start_other = gather(jnp.broadcast_to(psi[None], (SECS,) + psi.shape), FAR)
    base, size_of, masks, lefts, rights = call(
        prepare,
        (
            shape(SLOTS, LOCAL_TERMS, dtype=ints),
            shape(SECTORS, dtype=ints),
            shape(2, SLOTS, ROWS, WIDTH),
            env_shape,
            env_shape,
        ),
        (SMEM, SMEM, VMEM, VMEM, VMEM),
        (HBM,) * 3 + (VMEM,) * 2,
        scratch=(
            pltpu.SMEM((SLOTS, LOCAL_TERMS), ints),
            pltpu.SMEM((SECTORS,), ints),
            pltpu.SMEM((SECTORS,), ints),
            pltpu.SMEM((SECTORS,), ints),
            pltpu.SemaphoreType.DMA((3,)),
        ),
        flops=flops,
        moved=8 << 20,
    )(coupling, assign, sizes, left_env, right_env)
    parts = call(apply_first, shape(OPS, 2, SLOTS, ROWS, WIDTH), VMEM, (SMEM,) + (VMEM,) * 4, flops=flops)(
        base, start_mine, start_other, lefts, rights
    )
    parts = exchange(parts, SAME_SEC)
    sigma_first, copies = call(
        finish_first, (vec, shape(OPS, 2, SLOTS, ROWS, WIDTH)), (VMEM, VMEM), (VMEM, VMEM)
    )(masks, parts)
    mine, other = gather(copies, FAR_YZ)
    whole = shape(CHUNKS, ROWS, WIDTH)
    start_mine, start_other, sums = call(
        moments,
        (whole, whole, shape(2, ROWS, WIDTH)),
        (VMEM,) * 3,
        (SMEM,) + (VMEM,) * 3,
        flops=flops,
        aliases={1: 0, 2: 1},
    )(size_of, start_mine, start_other, mine)
    parts, next_vector = call(
        apply_next, (shape(OPS, SLOTS, ROWS, WIDTH), vec), (VMEM, VMEM), (SMEM,) + (VMEM,) * 10, flops=flops
    )(base, start_mine, start_other, mine, other, lefts, rights, psi, masks, sigma_first, sums)
    parts = exchange(parts, SAME_SEC)
    sigma_next = call(finish_next, vec, VMEM, (VMEM, VMEM))(masks, parts)
    return sigma_first, next_vector, sigma_next


def solution(mesh):
    placed = (
        P("sec", "op", None),
        P("op", "sec", None, None),
        P("op", "sec", None, None),
        P("sec", "op"),
        P(),
        P(),
    )
    return jax.shard_map(
        on_device,
        mesh=mesh,
        in_specs=placed,
        out_specs=(P("sec", "op", None),) * 3,
        check_vma=False,
    )
```

```python
import itertools

import jax
import jax.numpy as jnp
from jax import lax
from jax.experimental import pallas as pl
from jax.experimental.pallas import tpu as pltpu
from jax.sharding import PartitionSpec as P

AXES = ("op", "sec")
F32 = jnp.float32
BF16 = jnp.bfloat16
SLOTS, ROWS, WIDTH, LOCAL_TERMS = 2, 8, 128, 16
SECTORS = 64
OPS, SECS = 16, 32
CHUNKS = 512


PLACES = list(itertools.product(range(4), range(2), range(2), range(8), range(4)))


def number(x, zl, core, y, zh):
    return ((((x * 2 + zl) * 2 + core) * 8) + y) * 4 + zh


def groups(key, order):
    found = {}
    for place in PLACES:
        found.setdefault(key(*place), []).append((order(*place), number(*place)))
    return [[device for _, device in sorted(members)] for members in found.values()]


def cube(x, zl, core, y, zh):
    z = 2 * zh + zl
    return (x - core) % 4 // 2, (y - core) % 8 // 2, (z - core) % 8 // 2, core


SAME_SEC = groups(lambda x, zl, core, y, zh: (y, zh), lambda x, zl, core, y, zh: (x, zl, core))
FAR = groups(lambda x, zl, core, y, zh: (x % 2, y % 2, zl, core), lambda x, zl, core, y, zh: (y // 2, zh, x // 2))
FAR_YZ = groups(lambda x, zl, core, y, zh: (x, y % 2, zl, core), lambda x, zl, core, y, zh: (y // 2, zh))
NEAR = groups(cube, lambda x, zl, core, y, zh: (x % 2, y % 2, zl))
OTHER_CORE = [
    (number(x, zl, core, y, zh), number(x, zl, 1 - core, y, zh)) for x, zl, core, y, zh in PLACES
]
ROW_STEPS = [(x % 2) * 256 + zl * 64 + (x // 2) * 2 for x in range(4) for zl in range(2)]


def exchange(parts, members):
    return lax.all_to_all(parts, AXES, 0, 0, axis_index_groups=members)


VMEM = pl.BlockSpec(memory_space=pltpu.VMEM)
SMEM = pl.BlockSpec(memory_space=pltpu.SMEM)
HBM = pl.BlockSpec(memory_space=pltpu.HBM)


def call(body, outs, out_specs, in_specs, scratch=(), flops=0, moved=1 << 20):
    return pl.pallas_call(
        body,
        out_shape=outs,
        in_specs=in_specs,
        out_specs=out_specs,
        scratch_shapes=list(scratch),
        compiler_params=pltpu.CompilerParams(vmem_limit_bytes=40 << 20),
        cost_estimate=pl.CostEstimate(flops=flops, bytes_accessed=moved, transcendentals=0),
    )


def shape(*dims, dtype=F32):
    return jax.ShapeDtypeStruct(dims, dtype)


def inside(size, first_row):
    rows = first_row + lax.broadcasted_iota(jnp.int32, (ROWS, WIDTH), 0)
    cols = lax.broadcasted_iota(jnp.int32, (ROWS, WIDTH), 1)
    return (rows < size) & (cols < size)


def fetch(pairs, done):
    copies = [pltpu.make_async_copy(source, target, done.at[i]) for i, (source, target) in enumerate(pairs)]
    for copy in copies:
        copy.start()
    for copy in copies:
        copy.wait()


def halves(values):
    high = values.astype(BF16)
    return high, (values - high.astype(F32)).astype(BF16)


def prepare(
    coupling_hbm, assign_hbm, sizes_hbm, left, right, base, size_of, masks, lefts, rights, coupling, assign, sizes, slot_of, done
):
    fetch([(coupling_hbm, coupling), (assign_hbm, assign), (sizes_hbm, sizes)], done)
    op = lax.axis_index("op")
    for p in range(SECTORS):
        sector = assign[p]
        slot_of[sector] = p
        size_of[p] = sizes[sector]
    for t in range(SLOTS):
        for k in range(LOCAL_TERMS):
            p = slot_of[coupling[t, k]]
            y = p // 8
            base[t, k] = (y % 2) * 128 + (y // 2) * 16 + p % 8 // 2 * 4 + p % 2
        size = size_of[lax.axis_index("sec") * SLOTS + t]
        for xh in range(2):
            masks[xh, t] = inside(size, (xh * 8 + op % 8) * ROWS).astype(F32)
    row = lax.broadcasted_iota(jnp.int32, (WIDTH, WIDTH), 0)
    col = lax.broadcasted_iota(jnp.int32, (WIDTH, WIDTH), 1)
    other = (row // 8 % 2 != op % 2).astype(jnp.int32)
    order = (col == other * 64 + row // 16 * 8 + row % 8).astype(F32).astype(BF16)
    for k in range(LOCAL_TERMS):
        for t in range(SLOTS):
            size = sizes[coupling[t, k]]
            high, low = halves(jnp.where(col < size, left[k, t], 0.0))
            moved = matmul(jnp.concatenate([high, low], axis=0), order).astype(BF16)
            lefts[k, t, :, :WIDTH] = moved[:WIDTH]
            lefts[k, t, :, WIDTH:] = moved[WIDTH:]
            high, low = halves(jnp.where(col < size, right[k, t], 0.0).T)
            rights[k, t, :, :WIDTH] = high
            rights[k, t, :, WIDTH:] = low


def matmul(a, b):
    return lax.dot_general(a, b, (((1,), (0,)), ((), ())), preferred_element_type=F32)


def products(block_of, base, lefts, rights, store):
    results = []
    for t in range(SLOTS):
        total = jnp.zeros((WIDTH, 2 * WIDTH), F32)
        for k in range(LOCAL_TERMS):
            high, low = halves(block_of(base[t, k]))
            pair = jnp.concatenate([high, low], axis=1)
            inner = matmul(lefts[k, t], jnp.concatenate([pair, pair], axis=0))
            high, low = halves(inner[:, :WIDTH] + inner[:, WIDTH:])
            rows = rights[k, t]
            total = total + matmul(
                jnp.concatenate([high, low], axis=1), jnp.concatenate([rows, rows], axis=0)
            )
        results.append(total[:, :WIDTH] + total[:, WIDTH:])
    for t in range(SLOTS):
        for i in range(OPS):
            store(i, t, results[t][i * ROWS : (i + 1) * ROWS])


def gathered_block(mine, other, first):
    return jnp.concatenate(
        [mine[first + step] for step in ROW_STEPS] + [other[first + step] for step in ROW_STEPS], axis=0
    )


def apply_first(base, mine, other, lefts, rights, out):
    def store(i, t, rows):
        for x in range(2):
            out[x * 8 + i % 8, i // 8, t] = rows

    products(lambda first: gathered_block(mine, other, first), base, lefts, rights, store)


def finish_first(masks, parts, sigma, copies):
    mine = lax.axis_index("op") // 8
    for xh in range(2):
        for t in range(SLOTS):
            total = parts[0, xh, t]
            for i in range(1, OPS):
                total = total + parts[i, xh, t]
            total = total * masks[xh, t]
            for i in range(OPS):
                copies[i, xh, t] = total
    for t in range(SLOTS):
        sigma[t] = copies[0, mine, t]


LANES = 4


def whole_sum(values):
    return jnp.sum(jnp.sum(values, axis=1, keepdims=True), axis=0, keepdims=True)


def scan(step, count):
    def body(i, sums):
        sums = list(sums)
        for u in range(16):
            for n, term in enumerate(step(i, u)):
                at = n * LANES + u % LANES
                sums[at] = sums[at] + term
        return tuple(sums)

    zero = jnp.zeros((ROWS, WIDTH), F32)
    sums = lax.fori_loop(0, CHUNKS // 16, body, (zero,) * (count * LANES))
    return [whole_sum(sum(sums[n : n + LANES])) for n in range(0, len(sums), LANES)]


def moments(size_of, start, field, sums, masked):
    core = lax.axis_index("op") % 2
    rows = lax.broadcasted_iota(jnp.int32, (ROWS, WIDTH), 0)
    cols = lax.broadcasted_iota(jnp.int32, (ROWS, WIDTH), 1)

    def first(i, u):
        xl, yl, zl, yh = i // 16, i // 8 % 2, i // 4 % 2, i % 4
        zh, xh, t = u // 4, u // 2 % 2, u % 2
        size = size_of[(yh * 2 + yl) * 8 + zh * 2 + t]
        row_group = (xh * 4 + xl * 2 + zl) * 2 + core
        here = i * 16 + u
        s = jnp.where((cols < size) & (rows < size - row_group * ROWS), start[here], 0.0)
        masked[here] = s
        return s * field[here], s * s

    cross, square = scan(first, 2)
    theta = jnp.where(square > 0.0, cross / jnp.where(square > 0.0, square, 1.0), 0.0)

    def second(i, u):
        r = field[i * 16 + u] - theta * masked[i * 16 + u]
        return (r * r,)

    (left,) = scan(second, 1)
    sums[...] = jnp.where(rows == 0, cross, jnp.where(rows == 1, square, left))


def apply_next(base, mine, other, lefts, rights, sums, out):
    def store(i, t, rows):
        out[i, t] = rows

    products(lambda first: gathered_block(mine, other, first), base, lefts, rights, store)
    for i in range(OPS):
        out[i, SLOTS] = sums[...]


def finish_next(masks, parts, psi, sigma, next_vector, sigma_next):
    op = lax.axis_index("op")
    halves_sums = [parts[op - op % 2 + core, SLOTS] for core in range(2)]
    cross, square, left = zip(*[(h[0:1, 0:1], h[1:2, 0:1], h[2:3, 0:1]) for h in halves_sums])
    theta = (cross[0] + cross[1]) / (square[0] + square[1])
    norm = left[0] + left[1]
    for c, q in zip(cross, square):
        shift = jnp.where(q > 0.0, c / jnp.where(q > 0.0, q, 1.0), 0.0) - theta
        norm = norm + shift * q * shift
    scale = 1.0 / jnp.sqrt(norm + 1e-06)
    for t in range(SLOTS):
        total = parts[0, t]
        for i in range(1, OPS):
            total = total + parts[i, t]
        mask = masks[op // 8, t]
        sigma_next[t] = (total * mask - theta * sigma[t]) * scale
        next_vector[t] = (sigma[t] - theta * (psi[t] * mask)) * scale


def gather(copies, far):
    part = exchange(copies, far).reshape(1, CHUNKS // 8, ROWS, WIDTH)
    part = jnp.broadcast_to(part, (8, CHUNKS // 8, ROWS, WIDTH))
    mine = exchange(part, NEAR).reshape(CHUNKS, ROWS, WIDTH)
    return mine, lax.ppermute(mine, AXES, OTHER_CORE)


def on_device(psi, left_env, right_env, coupling, assign, sizes):
    ints = jnp.int32
    vec = shape(SLOTS, ROWS, WIDTH)
    env_shape = shape(LOCAL_TERMS, SLOTS, WIDTH, 2 * WIDTH, dtype=BF16)
    flops = 2 * 2 * 32 * 128 * 256 * 256

    start_mine, start_other = gather(jnp.broadcast_to(psi[None], (SECS,) + psi.shape), FAR)
    base, size_of, masks, lefts, rights = call(
        prepare,
        (
            shape(SLOTS, LOCAL_TERMS, dtype=ints),
            shape(SECTORS, dtype=ints),
            shape(2, SLOTS, ROWS, WIDTH),
            env_shape,
            env_shape,
        ),
        (SMEM, SMEM, VMEM, VMEM, VMEM),
        (HBM,) * 3 + (VMEM,) * 2,
        scratch=(
            pltpu.SMEM((SLOTS, LOCAL_TERMS), ints),
            pltpu.SMEM((SECTORS,), ints),
            pltpu.SMEM((SECTORS,), ints),
            pltpu.SMEM((SECTORS,), ints),
            pltpu.SemaphoreType.DMA((3,)),
        ),
        flops=flops,
        moved=8 << 20,
    )(coupling, assign, sizes, left_env, right_env)
    parts = call(apply_first, shape(OPS, 2, SLOTS, ROWS, WIDTH), VMEM, (SMEM,) + (VMEM,) * 4, flops=flops)(
        base, start_mine, start_other, lefts, rights
    )
    parts = exchange(parts, SAME_SEC)
    sigma_first, copies = call(
        finish_first, (vec, shape(OPS, 2, SLOTS, ROWS, WIDTH)), (VMEM, VMEM), (VMEM, VMEM)
    )(masks, parts)
    mine, other = gather(copies, FAR_YZ)
    sums = call(
        moments,
        shape(ROWS, WIDTH),
        VMEM,
        (SMEM, VMEM, VMEM),
        scratch=(pltpu.VMEM((CHUNKS, ROWS, WIDTH), F32),),
        flops=flops,
    )(size_of, start_mine, mine)
    parts = call(apply_next, shape(OPS, SLOTS + 1, ROWS, WIDTH), VMEM, (SMEM,) + (VMEM,) * 5, flops=flops)(
        base, mine, other, lefts, rights, sums
    )
    parts = exchange(parts, SAME_SEC)
    next_vector, sigma_next = call(finish_next, (vec, vec), (VMEM, VMEM), (VMEM,) * 4)(
        masks, parts, psi, sigma_first
    )
    return sigma_first, next_vector, sigma_next


def solution(mesh):
    placed = (
        P("sec", "op", None),
        P("op", "sec", None, None),
        P("op", "sec", None, None),
        P("sec", "op"),
        P(),
        P(),
    )
    return jax.shard_map(
        on_device,
        mesh=mesh,
        in_specs=placed,
        out_specs=(P("sec", "op", None),) * 3,
        check_vma=False,
    )
```

```python
import itertools

import jax
import jax.numpy as jnp
from jax import lax
from jax.experimental import pallas as pl
from jax.experimental.pallas import tpu as pltpu
from jax.sharding import PartitionSpec as P

AXES = ("op", "sec")
F32 = jnp.float32
BF16 = jnp.bfloat16
SLOTS, ROWS, WIDTH, LOCAL_TERMS = 2, 8, 128, 16
SECTORS = 64
OPS, SECS = 16, 32
CHUNKS = 512


PLACES = list(itertools.product(range(4), range(2), range(2), range(8), range(4)))


def number(x, zl, core, y, zh):
    return ((((x * 2 + zl) * 2 + core) * 8) + y) * 4 + zh


def groups(key, order):
    found = {}
    for place in PLACES:
        found.setdefault(key(*place), []).append((order(*place), number(*place)))
    return [[device for _, device in sorted(members)] for members in found.values()]


def cube(x, zl, core, y, zh):
    z = 2 * zh + zl
    return (x - core) % 4 // 2, (y - core) % 8 // 2, (z - core) % 8 // 2, core


SAME_SEC = groups(lambda x, zl, core, y, zh: (y, zh), lambda x, zl, core, y, zh: (x, zl, core))
FAR = groups(lambda x, zl, core, y, zh: (x % 2, y % 2, zl, core), lambda x, zl, core, y, zh: (y // 2, zh, x // 2))
FAR_YZ = groups(lambda x, zl, core, y, zh: (x, y % 2, zl, core), lambda x, zl, core, y, zh: (y // 2, zh))
NEAR = groups(cube, lambda x, zl, core, y, zh: (x % 2, y % 2, zl))
OTHER_CORE = [
    (number(x, zl, core, y, zh), number(x, zl, 1 - core, y, zh)) for x, zl, core, y, zh in PLACES
]
ROW_STEPS = [(x % 2) * 256 + zl * 64 + (x // 2) * 2 for x in range(4) for zl in range(2)]


def exchange(parts, members):
    return lax.all_to_all(parts, AXES, 0, 0, axis_index_groups=members)


VMEM = pl.BlockSpec(memory_space=pltpu.VMEM)
SMEM = pl.BlockSpec(memory_space=pltpu.SMEM)
HBM = pl.BlockSpec(memory_space=pltpu.HBM)


def call(body, outs, out_specs, in_specs, scratch=(), flops=0, moved=1 << 20):
    return pl.pallas_call(
        body,
        out_shape=outs,
        in_specs=in_specs,
        out_specs=out_specs,
        scratch_shapes=list(scratch),
        compiler_params=pltpu.CompilerParams(vmem_limit_bytes=40 << 20),
        cost_estimate=pl.CostEstimate(flops=flops, bytes_accessed=moved, transcendentals=0),
    )


def shape(*dims, dtype=F32):
    return jax.ShapeDtypeStruct(dims, dtype)


def inside(size, first_row):
    rows = first_row + lax.broadcasted_iota(jnp.int32, (ROWS, WIDTH), 0)
    cols = lax.broadcasted_iota(jnp.int32, (ROWS, WIDTH), 1)
    return (rows < size) & (cols < size)


def fetch(pairs, done):
    copies = [pltpu.make_async_copy(source, target, done.at[i]) for i, (source, target) in enumerate(pairs)]
    for copy in copies:
        copy.start()
    for copy in copies:
        copy.wait()


def halves(values):
    high = values.astype(BF16)
    return high, (values - high.astype(F32)).astype(BF16)


def prepare(
    coupling_hbm, assign_hbm, sizes_hbm, left, right, base, bases, size_of, masks, lefts, rights, coupling, assign, sizes, slot_of, done
):
    fetch([(coupling_hbm, coupling), (assign_hbm, assign), (sizes_hbm, sizes)], done)
    op = lax.axis_index("op")
    sub = lax.broadcasted_iota(jnp.int32, (ROWS, WIDTH), 0)
    lane = lax.broadcasted_iota(jnp.int32, (ROWS, WIDTH), 1)
    table = jnp.zeros((ROWS, WIDTH), jnp.int32)
    for p in range(SECTORS):
        sector = assign[p]
        slot_of[sector] = p
        size_of[p] = sizes[sector]
    for t in range(SLOTS):
        for k in range(LOCAL_TERMS):
            p = slot_of[coupling[t, k]]
            y = p // 8
            first = (y % 2) * 128 + (y // 2) * 16 + p % 8 // 2 * 4 + p % 2
            base[t, k] = first
            table = jnp.where((sub == t) & (lane == k), first, table)
        size = size_of[lax.axis_index("sec") * SLOTS + t]
        for xh in range(2):
            masks[xh, t] = inside(size, (xh * 8 + op % 8) * ROWS).astype(F32)
    bases[...] = table.astype(F32)
    row = lax.broadcasted_iota(jnp.int32, (WIDTH, WIDTH), 0)
    col = lax.broadcasted_iota(jnp.int32, (WIDTH, WIDTH), 1)
    other = (row // 8 % 2 != op % 2).astype(jnp.int32)
    order = (col == other * 64 + row // 16 * 8 + row % 8).astype(F32).astype(BF16)
    for k in range(LOCAL_TERMS):
        for t in range(SLOTS):
            size = sizes[coupling[t, k]]
            high, low = halves(jnp.where(col < size, left[k, t], 0.0))
            moved = matmul(jnp.concatenate([high, low], axis=0), order).astype(BF16)
            lefts[k, t, :, :WIDTH] = moved[:WIDTH]
            lefts[k, t, :, WIDTH:] = moved[WIDTH:]
            high, low = halves(jnp.where(col < size, right[k, t], 0.0).T)
            rights[k, t, :, :WIDTH] = high
            rights[k, t, :, WIDTH:] = low


def matmul(a, b):
    return lax.dot_general(a, b, (((1,), (0,)), ((), ())), preferred_element_type=F32)


def products(block_of, lefts, rights, store):
    results = []
    for t in range(SLOTS):
        total = jnp.zeros((WIDTH, 2 * WIDTH), F32)
        for k in range(LOCAL_TERMS):
            high, low = halves(block_of(t, k))
            pair = jnp.concatenate([high, low], axis=1)
            inner = matmul(lefts[k, t], jnp.concatenate([pair, pair], axis=0))
            high, low = halves(inner[:, :WIDTH] + inner[:, WIDTH:])
            rows = rights[k, t]
            total = total + matmul(
                jnp.concatenate([high, low], axis=1), jnp.concatenate([rows, rows], axis=0)
            )
        results.append(total[:, :WIDTH] + total[:, WIDTH:])
    for t in range(SLOTS):
        for i in range(OPS):
            store(i, t, results[t][i * ROWS : (i + 1) * ROWS])


def own_rows(field, first):
    return [field[first + step] for step in ROW_STEPS]


def gathered_block(mine, other, first):
    return jnp.concatenate(own_rows(mine, first) + own_rows(other, first), axis=0)


def apply_first(base, bases, mine, other, lefts, rights, out):
    def store(i, t, rows):
        for x in range(2):
            out[x * 8 + i % 8, i // 8 * SLOTS + t] = rows

    products(lambda t, k: gathered_block(mine, other, base[t, k]), lefts, rights, store)
    for i in range(OPS):
        out[i, 2 * SLOTS] = bases[...]


def finish_first(masks, parts, sigma, copies, other_base):
    op = lax.axis_index("op")
    for xh in range(2):
        for t in range(SLOTS):
            total = parts[0, xh * SLOTS + t]
            for i in range(1, OPS):
                total = total + parts[i, xh * SLOTS + t]
            total = total * masks[xh, t]
            for i in range(OPS):
                copies[i, xh, t] = total
    for t in range(SLOTS):
        sigma[t] = copies[0, op // 8, t]
    other_base[...] = parts[op + 1 - 2 * (op % 2), 2 * SLOTS].astype(jnp.int32)


def pack(other_base, mine, packed):
    for t in range(SLOTS):
        for k in range(LOCAL_TERMS):
            first = other_base[t, k]
            for n, step in enumerate(ROW_STEPS):
                packed[t, k, n] = mine[first + step]


LANES = 4


def whole_sum(values):
    return jnp.sum(jnp.sum(values, axis=1, keepdims=True), axis=0, keepdims=True)


def scan(step, count):
    op = lax.axis_index("op")
    start = op // 4 % 2 * 256 + op // 2 % 2 * 64

    def body(i, sums):
        sums = list(sums)
        for yl in range(2):
            for u in range(16):
                for n, term in enumerate(step(yl, i, u, start + yl * 128 + i * 16 + u)):
                    at = n * LANES + u % LANES
                    sums[at] = sums[at] + term
        return tuple(sums)

    zero = jnp.zeros((ROWS, WIDTH), F32)
    sums = lax.fori_loop(0, 4, body, (zero,) * (count * LANES))
    return [whole_sum(sum(sums[n : n + LANES])) for n in range(0, len(sums), LANES)]


def projection(cross, square):
    some = square > 0.0
    return jnp.where(some, cross / jnp.where(some, square, 1.0), 0.0)


def moments(size_of, start, field, sums, masked):
    op = lax.axis_index("op")
    rows = lax.broadcasted_iota(jnp.int32, (ROWS, WIDTH), 0)
    cols = lax.broadcasted_iota(jnp.int32, (ROWS, WIDTH), 1)

    def first(yl, yh, u, here):
        zh, xh, t = u // 4, u // 2 % 2, u % 2
        size = size_of[(yh * 2 + yl) * 8 + zh * 2 + t]
        s = jnp.where((cols < size) & (rows < size - (xh * 8 + op % 8) * ROWS), start[here], 0.0)
        masked[yl * 64 + yh * 16 + u] = s
        return s * field[here], s * s

    cross, square = scan(first, 2)
    theta = projection(cross, square)

    def second(yl, yh, u, here):
        r = field[here] - theta * masked[yl * 64 + yh * 16 + u]
        return (r * r,)

    (left,) = scan(second, 1)
    sums[...] = jnp.where(rows == 0, cross, jnp.where(rows == 1, square, left))


def apply_next(base, mine, packed, lefts, rights, sums, out):
    def block(t, k):
        other = [packed[t, k, n] for n in range(len(ROW_STEPS))]
        return jnp.concatenate(own_rows(mine, base[t, k]) + other, axis=0)

    def store(i, t, rows):
        out[i, t] = rows

    products(block, lefts, rights, store)
    for i in range(OPS):
        out[i, SLOTS] = sums[...]


def finish_next(masks, parts, psi, sigma, next_vector, sigma_next):
    xh = lax.axis_index("op") // 8
    cross, square, left = [
        jnp.concatenate([parts[xh * 8 + i, SLOTS, n : n + 1] for i in range(8)], axis=0) for n in range(3)
    ]
    theta = jnp.sum(cross, axis=0, keepdims=True) / jnp.sum(square, axis=0, keepdims=True)
    shift = projection(cross, square) - theta
    norm = jnp.sum(left + shift * square * shift, axis=0, keepdims=True)
    scale = 1.0 / jnp.sqrt(norm + 1e-06)
    for t in range(SLOTS):
        total = parts[0, t]
        for i in range(1, OPS):
            total = total + parts[i, t]
        mask = masks[xh, t]
        sigma_next[t] = (total * mask - theta * sigma[t]) * scale
        next_vector[t] = (sigma[t] - theta * (psi[t] * mask)) * scale


def gather(copies, far):
    part = exchange(copies, far).reshape(1, CHUNKS // 8, ROWS, WIDTH)
    part = jnp.broadcast_to(part, (8, CHUNKS // 8, ROWS, WIDTH))
    return exchange(part, NEAR).reshape(CHUNKS, ROWS, WIDTH)


def on_device(psi, left_env, right_env, coupling, assign, sizes):
    ints = jnp.int32
    vec = shape(SLOTS, ROWS, WIDTH)
    chunk = shape(ROWS, WIDTH)
    env_shape = shape(LOCAL_TERMS, SLOTS, WIDTH, 2 * WIDTH, dtype=BF16)
    flops = 2 * 2 * 32 * 128 * 256 * 256

    start_mine = gather(jnp.broadcast_to(psi[None], (SECS,) + psi.shape), FAR)
    start_other = lax.ppermute(start_mine, AXES, OTHER_CORE)
    base, bases, size_of, masks, lefts, rights = call(
        prepare,
        (
            shape(SLOTS, LOCAL_TERMS, dtype=ints),
            chunk,
            shape(SECTORS, dtype=ints),
            shape(2, SLOTS, ROWS, WIDTH),
            env_shape,
            env_shape,
        ),
        (SMEM, VMEM, SMEM, VMEM, VMEM, VMEM),
        (HBM,) * 3 + (VMEM,) * 2,
        scratch=(
            pltpu.SMEM((SLOTS, LOCAL_TERMS), ints),
            pltpu.SMEM((SECTORS,), ints),
            pltpu.SMEM((SECTORS,), ints),
            pltpu.SMEM((SECTORS,), ints),
            pltpu.SemaphoreType.DMA((3,)),
        ),
        flops=flops,
        moved=8 << 20,
    )(coupling, assign, sizes, left_env, right_env)
    parts = call(apply_first, shape(OPS, 2 * SLOTS + 1, ROWS, WIDTH), VMEM, (SMEM,) + (VMEM,) * 5, flops=flops)(
        base, bases, start_mine, start_other, lefts, rights
    )
    parts = exchange(parts, SAME_SEC)
    sigma_first, copies, other_base = call(
        finish_first,
        (vec, shape(OPS, 2, SLOTS, ROWS, WIDTH), shape(ROWS, WIDTH, dtype=ints)),
        (VMEM,) * 3,
        (VMEM, VMEM),
    )(masks, parts)
    mine = gather(copies, FAR_YZ)
    packed = call(pack, shape(SLOTS, LOCAL_TERMS, len(ROW_STEPS), ROWS, WIDTH), VMEM, (SMEM, VMEM))(
        other_base[:SLOTS, :LOCAL_TERMS], mine
    )
    other = lax.ppermute(packed, AXES, OTHER_CORE)
    sums = call(
        moments,
        chunk,
        VMEM,
        (SMEM, VMEM, VMEM),
        scratch=(pltpu.VMEM((CHUNKS // 4, ROWS, WIDTH), F32),),
        flops=flops,
    )(size_of, start_mine, mine)
    parts = call(apply_next, shape(OPS, SLOTS + 1, ROWS, WIDTH), VMEM, (SMEM,) + (VMEM,) * 5, flops=flops)(
        base, mine, other, lefts, rights, sums
    )
    parts = exchange(parts, SAME_SEC)
    next_vector, sigma_next = call(finish_next, (vec, vec), (VMEM, VMEM), (VMEM,) * 4)(
        masks, parts, psi, sigma_first
    )
    return sigma_first, next_vector, sigma_next


def solution(mesh):
    placed = (
        P("sec", "op", None),
        P("op", "sec", None, None),
        P("op", "sec", None, None),
        P("sec", "op"),
        P(),
        P(),
    )
    return jax.shard_map(
        on_device,
        mesh=mesh,
        in_specs=placed,
        out_specs=(P("sec", "op", None),) * 3,
        check_vma=False,
    )
```

```python
import itertools

import jax
import jax.numpy as jnp
from jax import lax
from jax.experimental import pallas as pl
from jax.experimental.pallas import tpu as pltpu
from jax.sharding import PartitionSpec as P

AXES = ("op", "sec")
F32 = jnp.float32
BF16 = jnp.bfloat16
SLOTS, ROWS, WIDTH, LOCAL_TERMS = 2, 8, 128, 16
SECTORS = 64
OPS, SECS = 16, 32
CHUNKS = 512


PLACES = list(itertools.product(range(4), range(2), range(2), range(8), range(4)))


def number(x, zl, core, y, zh):
    return ((((x * 2 + zl) * 2 + core) * 8) + y) * 4 + zh


def groups(key, order):
    found = {}
    for place in PLACES:
        found.setdefault(key(*place), []).append((order(*place), number(*place)))
    return [[device for _, device in sorted(members)] for members in found.values()]


def cube(x, zl, core, y, zh):
    z = 2 * zh + zl
    return (x - core) % 4 // 2, (y - core) % 8 // 2, (z - core) % 8 // 2, core


SAME_SEC = groups(lambda x, zl, core, y, zh: (y, zh), lambda x, zl, core, y, zh: (x, zl, core))
FAR = groups(lambda x, zl, core, y, zh: (x % 2, y % 2, zl, core), lambda x, zl, core, y, zh: (y // 2, zh, x // 2))
FAR_YZ = groups(lambda x, zl, core, y, zh: (x, y % 2, zl, core), lambda x, zl, core, y, zh: (y // 2, zh))
NEAR = groups(cube, lambda x, zl, core, y, zh: (x % 2, y % 2, zl))
OTHER_CORE = [
    (number(x, zl, core, y, zh), number(x, zl, 1 - core, y, zh)) for x, zl, core, y, zh in PLACES
]
ROW_STEPS = [(x % 2) * 256 + zl * 64 + (x // 2) * 2 for x in range(4) for zl in range(2)]


def exchange(parts, members):
    return lax.all_to_all(parts, AXES, 0, 0, axis_index_groups=members)


VMEM = pl.BlockSpec(memory_space=pltpu.VMEM)
SMEM = pl.BlockSpec(memory_space=pltpu.SMEM)
HBM = pl.BlockSpec(memory_space=pltpu.HBM)


def call(body, outs, out_specs, in_specs, scratch=(), flops=0, moved=1 << 20):
    return pl.pallas_call(
        body,
        out_shape=outs,
        in_specs=in_specs,
        out_specs=out_specs,
        scratch_shapes=list(scratch),
        compiler_params=pltpu.CompilerParams(vmem_limit_bytes=40 << 20),
        cost_estimate=pl.CostEstimate(flops=flops, bytes_accessed=moved, transcendentals=0),
    )


def shape(*dims, dtype=F32):
    return jax.ShapeDtypeStruct(dims, dtype)


def inside(size, first_row):
    rows = first_row + lax.broadcasted_iota(jnp.int32, (ROWS, WIDTH), 0)
    cols = lax.broadcasted_iota(jnp.int32, (ROWS, WIDTH), 1)
    return (rows < size) & (cols < size)


def fetch(pairs, done):
    copies = [pltpu.make_async_copy(source, target, done.at[i]) for i, (source, target) in enumerate(pairs)]
    for copy in copies:
        copy.start()
    for copy in copies:
        copy.wait()


def halves(values):
    high = values.astype(BF16)
    return high, (values - high.astype(F32)).astype(BF16)


def prepare(
    coupling_hbm, assign_hbm, sizes_hbm, left, right, base, bases, size_of, masks, lefts, rights, coupling, assign, sizes, slot_of, done
):
    fetch([(coupling_hbm, coupling), (assign_hbm, assign), (sizes_hbm, sizes)], done)
    op = lax.axis_index("op")
    sub = lax.broadcasted_iota(jnp.int32, (ROWS, WIDTH), 0)
    lane = lax.broadcasted_iota(jnp.int32, (ROWS, WIDTH), 1)
    table = jnp.zeros((ROWS, WIDTH), jnp.int32)
    for p in range(SECTORS):
        sector = assign[p]
        slot_of[sector] = p
        size_of[p] = sizes[sector]
    for t in range(SLOTS):
        for k in range(LOCAL_TERMS):
            p = slot_of[coupling[t, k]]
            y = p // 8
            first = (y % 2) * 128 + (y // 2) * 16 + p % 8 // 2 * 4 + p % 2
            base[t, k] = first
            table = jnp.where((sub == t) & (lane == k), first, table)
        size = size_of[lax.axis_index("sec") * SLOTS + t]
        for xh in range(2):
            masks[xh, t] = inside(size, (xh * 8 + op % 8) * ROWS).astype(F32)
    bases[...] = table.astype(F32)
    row = lax.broadcasted_iota(jnp.int32, (WIDTH, WIDTH), 0)
    col = lax.broadcasted_iota(jnp.int32, (WIDTH, WIDTH), 1)
    other = (row // 8 % 2 != op % 2).astype(jnp.int32)
    order = (col == other * 64 + row // 16 * 8 + row % 8).astype(F32).astype(BF16)
    for k in range(LOCAL_TERMS):
        for t in range(SLOTS):
            size = sizes[coupling[t, k]]
            high, low = halves(jnp.where(col < size, left[k, t], 0.0))
            moved = matmul(jnp.concatenate([high, low], axis=0), order).astype(BF16)
            lefts[k, t, :, :WIDTH] = moved[:WIDTH]
            lefts[k, t, :, WIDTH:] = moved[WIDTH:]
            high, low = halves(jnp.where(col < size, right[k, t], 0.0).T)
            rights[k, t, :, :WIDTH] = high
            rights[k, t, :, WIDTH:] = low


def matmul(a, b):
    return lax.dot_general(a, b, (((1,), (0,)), ((), ())), preferred_element_type=F32)


def products(block_of, lefts, rights, store):
    results = []
    for t in range(SLOTS):
        total = jnp.zeros((WIDTH, 2 * WIDTH), F32)
        for k in range(LOCAL_TERMS):
            high, low = halves(block_of(t, k))
            pair = jnp.concatenate([high, low], axis=1)
            inner = matmul(lefts[k, t], jnp.concatenate([pair, pair], axis=0))
            high, low = halves(inner[:, :WIDTH] + inner[:, WIDTH:])
            rows = rights[k, t]
            total = total + matmul(
                jnp.concatenate([high, low], axis=1), jnp.concatenate([rows, rows], axis=0)
            )
        results.append(total[:, :WIDTH] + total[:, WIDTH:])
    for t in range(SLOTS):
        for i in range(OPS):
            store(i, t, results[t][i * ROWS : (i + 1) * ROWS])


def own_rows(field, first):
    return [field[first + step] for step in ROW_STEPS]


def gathered_block(mine, other, first):
    return jnp.concatenate(own_rows(mine, first) + own_rows(other, first), axis=0)


def apply_first(base, bases, mine, other, lefts, rights, out):
    def store(i, t, rows):
        for x in range(2):
            out[x * 8 + i % 8, i // 8 * SLOTS + t] = rows

    products(lambda t, k: gathered_block(mine, other, base[t, k]), lefts, rights, store)
    for i in range(OPS):
        out[i, 2 * SLOTS] = bases[...]


def finish_first(masks, parts, sigma, copies, other_base):
    op = lax.axis_index("op")
    for xh in range(2):
        for t in range(SLOTS):
            total = parts[0, xh * SLOTS + t]
            for i in range(1, OPS):
                total = total + parts[i, xh * SLOTS + t]
            total = total * masks[xh, t]
            for i in range(OPS):
                copies[i, xh, t] = total
    for t in range(SLOTS):
        sigma[t] = copies[0, op // 8, t]
    other_base[...] = parts[op + 1 - 2 * (op % 2), 2 * SLOTS].astype(jnp.int32)


def pack(other_base, mine, packed):
    for t in range(SLOTS):
        for k in range(LOCAL_TERMS):
            first = other_base[t, k]
            for n, step in enumerate(ROW_STEPS):
                packed[t, k, n] = mine[first + step]


LANES = 4


def whole_sum(values):
    return jnp.sum(jnp.sum(values, axis=1, keepdims=True), axis=0, keepdims=True)


def scan(step, count):
    op = lax.axis_index("op")
    start = op // 4 % 2 * 256 + op // 2 % 2 * 64

    def body(i, sums):
        sums = list(sums)
        for yl in range(2):
            for u in range(16):
                for n, term in enumerate(step(yl, i, u, start + yl * 128 + i * 16 + u)):
                    at = n * LANES + u % LANES
                    sums[at] = sums[at] + term
        return tuple(sums)

    zero = jnp.zeros((ROWS, WIDTH), F32)
    sums = lax.fori_loop(0, 4, body, (zero,) * (count * LANES))
    return [whole_sum(sum(sums[n : n + LANES])) for n in range(0, len(sums), LANES)]


def projection(cross, square):
    some = square > 0.0
    return jnp.where(some, cross / jnp.where(some, square, 1.0), 0.0)


def moments(size_of, start, field, sums, masked):
    op = lax.axis_index("op")
    rows = lax.broadcasted_iota(jnp.int32, (ROWS, WIDTH), 0)
    cols = lax.broadcasted_iota(jnp.int32, (ROWS, WIDTH), 1)

    def first(yl, yh, u, here):
        zh, xh, t = u // 4, u // 2 % 2, u % 2
        size = size_of[(yh * 2 + yl) * 8 + zh * 2 + t]
        s = jnp.where((cols < size) & (rows < size - (xh * 8 + op % 8) * ROWS), start[here], 0.0)
        masked[yl * 64 + yh * 16 + u] = s
        return s * field[here], s * s

    cross, square = scan(first, 2)
    theta = projection(cross, square)

    def second(yl, yh, u, here):
        r = field[here] - theta * masked[yl * 64 + yh * 16 + u]
        return (r * r,)

    (left,) = scan(second, 1)
    sums[...] = jnp.where(rows == 0, cross, jnp.where(rows == 1, square, left))


def apply_next(base, mine, packed, lefts, rights, sums, out):
    def block(t, k):
        other = [packed[t, k, n] for n in range(len(ROW_STEPS))]
        return jnp.concatenate(own_rows(mine, base[t, k]) + other, axis=0)

    def store(i, t, rows):
        out[i, t] = rows

    products(block, lefts, rights, store)
    for i in range(OPS):
        out[i, SLOTS] = sums[...]


def finish_next(masks, parts, psi, sigma, next_vector, sigma_next):
    xh = lax.axis_index("op") // 8
    cross, square, left = [
        jnp.concatenate([parts[xh * 8 + i, SLOTS, n : n + 1] for i in range(8)], axis=0) for n in range(3)
    ]
    theta = jnp.sum(cross, axis=0, keepdims=True) / jnp.sum(square, axis=0, keepdims=True)
    shift = projection(cross, square) - theta
    norm = jnp.sum(left + shift * square * shift, axis=0, keepdims=True)
    scale = 1.0 / jnp.sqrt(norm + 1e-06)
    for t in range(SLOTS):
        total = parts[0, t]
        for i in range(1, OPS):
            total = total + parts[i, t]
        mask = masks[xh, t]
        sigma_next[t] = (total * mask - theta * sigma[t]) * scale
        next_vector[t] = (sigma[t] - theta * (psi[t] * mask)) * scale


def gather(copies, far):
    part = exchange(copies, far).reshape(1, CHUNKS // 8, ROWS, WIDTH)
    part = jnp.broadcast_to(part, (8, CHUNKS // 8, ROWS, WIDTH))
    return exchange(part, NEAR).reshape(CHUNKS, ROWS, WIDTH)


def on_device(psi, left_env, right_env, coupling, assign, sizes):
    ints = jnp.int32
    vec = shape(SLOTS, ROWS, WIDTH)
    chunk = shape(ROWS, WIDTH)
    env_shape = shape(LOCAL_TERMS, SLOTS, WIDTH, 2 * WIDTH, dtype=BF16)
    flops = 2 * 2 * 32 * 128 * 256 * 256

    start_mine = gather(jnp.broadcast_to(psi[None], (SECS,) + psi.shape), FAR)
    start_other = lax.ppermute(start_mine, AXES, OTHER_CORE)
    base, bases, size_of, masks, lefts, rights = call(
        prepare,
        (
            shape(SLOTS, LOCAL_TERMS, dtype=ints),
            chunk,
            shape(SECTORS, dtype=ints),
            shape(2, SLOTS, ROWS, WIDTH),
            env_shape,
            env_shape,
        ),
        (SMEM, VMEM, SMEM, VMEM, VMEM, VMEM),
        (HBM,) * 3 + (VMEM,) * 2,
        scratch=(
            pltpu.SMEM((SLOTS, LOCAL_TERMS), ints),
            pltpu.SMEM((SECTORS,), ints),
            pltpu.SMEM((SECTORS,), ints),
            pltpu.SMEM((SECTORS,), ints),
            pltpu.SemaphoreType.DMA((3,)),
        ),
        flops=flops,
        moved=8 << 20,
    )(coupling, assign, sizes, left_env, right_env)
    parts = call(apply_first, shape(OPS, 2 * SLOTS + 1, ROWS, WIDTH), VMEM, (SMEM,) + (VMEM,) * 5, flops=flops)(
        base, bases, start_mine, start_other, lefts, rights
    )
    parts = exchange(parts, SAME_SEC)
    sigma_first, copies, other_base = call(
        finish_first,
        (vec, shape(OPS, 2, SLOTS, ROWS, WIDTH), shape(ROWS, WIDTH, dtype=ints)),
        (VMEM,) * 3,
        (VMEM, VMEM),
    )(masks, parts)
    mine = gather(copies, FAR_YZ)
    packed = call(pack, shape(SLOTS, LOCAL_TERMS, len(ROW_STEPS), ROWS, WIDTH), VMEM, (SMEM, VMEM))(
        other_base, mine
    )
    other = lax.ppermute(packed, AXES, OTHER_CORE)
    sums = call(
        moments,
        chunk,
        VMEM,
        (SMEM, VMEM, VMEM),
        scratch=(pltpu.VMEM((CHUNKS // 4, ROWS, WIDTH), F32),),
        flops=flops,
    )(size_of, start_mine, mine)
    parts = call(apply_next, shape(OPS, SLOTS + 1, ROWS, WIDTH), VMEM, (SMEM,) + (VMEM,) * 5, flops=flops)(
        base, mine, other, lefts, rights, sums
    )
    parts = exchange(parts, SAME_SEC)
    next_vector, sigma_next = call(finish_next, (vec, vec), (VMEM, VMEM), (VMEM,) * 4)(
        masks, parts, psi, sigma_first
    )
    return sigma_first, next_vector, sigma_next


def solution(mesh):
    placed = (
        P("sec", "op", None),
        P("op", "sec", None, None),
        P("op", "sec", None, None),
        P("sec", "op"),
        P(),
        P(),
    )
    return jax.shard_map(
        on_device,
        mesh=mesh,
        in_specs=placed,
        out_specs=(P("sec", "op", None),) * 3,
        check_vma=False,
    )
```

```python
import itertools

import jax
import jax.numpy as jnp
from jax import lax
from jax.experimental import pallas as pl
from jax.experimental.pallas import tpu as pltpu
from jax.sharding import PartitionSpec as P

AXES = ("op", "sec")
F32 = jnp.float32
BF16 = jnp.bfloat16
SLOTS, ROWS, WIDTH, LOCAL_TERMS = 2, 8, 128, 16
SECTORS = 64
OPS, SECS = 16, 32
CHUNKS = 512


PLACES = list(itertools.product(range(4), range(2), range(2), range(8), range(4)))


def number(x, zl, core, y, zh):
    return ((((x * 2 + zl) * 2 + core) * 8) + y) * 4 + zh


def groups(key, order):
    found = {}
    for place in PLACES:
        found.setdefault(key(*place), []).append((order(*place), number(*place)))
    return [[device for _, device in sorted(members)] for members in found.values()]


def cube(x, zl, core, y, zh):
    z = 2 * zh + zl
    return (x - core) % 4 // 2, (y - core) % 8 // 2, (z - core) % 8 // 2, core


def kind(x, zl, core, y, zh):
    return (x + 2 * zl) % 4 * 2 + (y + zl) % 2


SAME_SEC = groups(lambda x, zl, core, y, zh: (y, zh), lambda x, zl, core, y, zh: (x, zl, core))
FAR = groups(lambda *place: (kind(*place), place[2]), lambda x, zl, core, y, zh: (zh, zl, y // 2))
NEAR = groups(cube, kind)
OTHER_CORE = [
    (number(x, zl, core, y, zh), number(x, zl, 1 - core, y, zh)) for x, zl, core, y, zh in PLACES
]


def exchange(parts, members):
    return lax.all_to_all(parts, AXES, 0, 0, axis_index_groups=members)


VMEM = pl.BlockSpec(memory_space=pltpu.VMEM)
SMEM = pl.BlockSpec(memory_space=pltpu.SMEM)
HBM = pl.BlockSpec(memory_space=pltpu.HBM)


def call(body, outs, out_specs, in_specs, scratch=(), flops=0, moved=1 << 20):
    return pl.pallas_call(
        body,
        out_shape=outs,
        in_specs=in_specs,
        out_specs=out_specs,
        scratch_shapes=list(scratch),
        compiler_params=pltpu.CompilerParams(vmem_limit_bytes=40 << 20),
        cost_estimate=pl.CostEstimate(flops=flops, bytes_accessed=moved, transcendentals=0),
    )


def shape(*dims, dtype=F32):
    return jax.ShapeDtypeStruct(dims, dtype)


def inside(size, first_row):
    rows = first_row + lax.broadcasted_iota(jnp.int32, (ROWS, WIDTH), 0)
    cols = lax.broadcasted_iota(jnp.int32, (ROWS, WIDTH), 1)
    return (rows < size) & (cols < size)


def fetch(pairs, done):
    copies = [pltpu.make_async_copy(source, target, done.at[i]) for i, (source, target) in enumerate(pairs)]
    for copy in copies:
        copy.start()
    for copy in copies:
        copy.wait()


def halves(values):
    high = values.astype(BF16)
    return high, (values - high.astype(F32)).astype(BF16)


def prepare(
    coupling_hbm, assign_hbm, sizes_hbm, left, right, base, bases, size_of, masks, lefts, rights, coupling, assign, sizes, slot_of, done
):
    fetch([(coupling_hbm, coupling), (assign_hbm, assign), (sizes_hbm, sizes)], done)
    op = lax.axis_index("op")
    sub = lax.broadcasted_iota(jnp.int32, (ROWS, WIDTH), 0)
    lane = lax.broadcasted_iota(jnp.int32, (ROWS, WIDTH), 1)
    table = jnp.zeros((ROWS, WIDTH), jnp.int32)
    for p in range(SECTORS):
        sector = assign[p]
        slot_of[sector] = p
        size_of[p] = sizes[sector]
    for t in range(SLOTS):
        for k in range(LOCAL_TERMS):
            p = slot_of[coupling[t, k]]
            y = p // 8
            first = y % 2 * 64 + p % 8 // 2 * 16 + y // 2 * 2 + p % 2
            base[t, k] = first
            table = jnp.where((sub == t) & (lane == k), first, table)
        masks[t] = inside(size_of[lax.axis_index("sec") * SLOTS + t], op * ROWS).astype(F32)
    bases[...] = table.astype(F32)
    row = lax.broadcasted_iota(jnp.int32, (WIDTH, WIDTH), 0)
    col = lax.broadcasted_iota(jnp.int32, (WIDTH, WIDTH), 1)
    other = (row // 8 % 2 != op % 2).astype(jnp.int32)
    order = (col == other * 64 + row // 16 * 8 + row % 8).astype(F32).astype(BF16)
    for k in range(LOCAL_TERMS):
        for t in range(SLOTS):
            size = sizes[coupling[t, k]]
            high, low = halves(jnp.where(col < size, left[k, t], 0.0))
            moved = matmul(jnp.concatenate([high, low], axis=0), order).astype(BF16)
            lefts[k, t, :, :WIDTH] = moved[:WIDTH]
            lefts[k, t, :, WIDTH:] = moved[WIDTH:]
            high, low = halves(jnp.where(col < size, right[k, t], 0.0).T)
            rights[k, t, :, :WIDTH] = high
            rights[k, t, :, WIDTH:] = low


def matmul(a, b):
    return lax.dot_general(a, b, (((1,), (0,)), ((), ())), preferred_element_type=F32)


def products(block_of, lefts, rights, store):
    results = []
    for t in range(SLOTS):
        total = jnp.zeros((WIDTH, 2 * WIDTH), F32)
        for k in range(LOCAL_TERMS):
            high, low = halves(block_of(t, k))
            pair = jnp.concatenate([high, low], axis=1)
            inner = matmul(lefts[k, t], jnp.concatenate([pair, pair], axis=0))
            high, low = halves(inner[:, :WIDTH] + inner[:, WIDTH:])
            rows = rights[k, t]
            total = total + matmul(
                jnp.concatenate([high, low], axis=1), jnp.concatenate([rows, rows], axis=0)
            )
        results.append(total[:, :WIDTH] + total[:, WIDTH:])
    for t in range(SLOTS):
        for i in range(OPS):
            store(i, t, results[t][i * ROWS : (i + 1) * ROWS])


def own_rows(field, first):
    starts = (first, first ^ 64)
    return [field[starts[zl] + ((x + 2 * zl) % 4 * 128 + zl * 8)] for x in range(4) for zl in range(2)]


def gathered_block(mine, other, first):
    return jnp.concatenate(own_rows(mine, first) + own_rows(other, first), axis=0)


def store_in(out):
    def store(i, t, rows):
        out[i, t] = rows

    return store


def apply_first(base, bases, mine, other, lefts, rights, out):
    products(lambda t, k: gathered_block(mine, other, base[t, k]), lefts, rights, store_in(out))
    for i in range(OPS):
        out[i, SLOTS] = bases[...]


def reduced(parts, t):
    total = parts[0, t]
    for i in range(1, OPS):
        total = total + parts[i, t]
    return total


def finish_first(masks, parts, sigma, copies, other_base):
    op = lax.axis_index("op")
    for t in range(SLOTS):
        total = reduced(parts, t) * masks[t]
        sigma[t] = total
        for i in range(SECS):
            copies[i, t] = total
    other_base[...] = parts[op + 1 - 2 * (op % 2), SLOTS].astype(jnp.int32)


def pack(other_base, mine, packed):
    for t in range(SLOTS):
        for k in range(LOCAL_TERMS):
            for n, chunk in enumerate(own_rows(mine, other_base[t, k])):
                packed[t, k, n] = chunk


LANES = 4


def whole_sum(values):
    return jnp.sum(jnp.sum(values, axis=1, keepdims=True), axis=0, keepdims=True)


def scan(step, count):
    x, zl = lax.axis_index("op") // 4, lax.axis_index("op") // 2 % 2
    start = (x + 2 * zl) % 4 * 128 + zl * 8
    sums = [jnp.zeros((ROWS, WIDTH), F32)] * (count * LANES)
    for u, (yl, zh, yh, t) in enumerate(itertools.product(range(2), range(4), range(4), range(2))):
        for n, term in enumerate(step(u, (yl, zh, yh, t), start + (yl * 64 + zh * 16 + yh * 2 + t))):
            at = n * LANES + u % LANES
            sums[at] = sums[at] + term
    return [whole_sum(sum(sums[n : n + LANES])) for n in range(0, len(sums), LANES)]


def projection(cross, square):
    some = square > 0.0
    return jnp.where(some, cross / jnp.where(some, square, 1.0), 0.0)


def moments(size_of, start, field, sums, masked):
    op = lax.axis_index("op")
    rows = lax.broadcasted_iota(jnp.int32, (ROWS, WIDTH), 0)
    cols = lax.broadcasted_iota(jnp.int32, (ROWS, WIDTH), 1)

    def first(u, where, here):
        yl, zh, yh, t = where
        y = yh * 2 + (yl + op // 2) % 2
        size = size_of[y * 8 + zh * 2 + t]
        s = jnp.where((cols < size) & (rows < size - op * ROWS), start[here], 0.0)
        masked[u] = s
        return s * field[here], s * s

    cross, square = scan(first, 2)
    theta = projection(cross, square)

    def second(u, where, here):
        r = field[here] - theta * masked[u]
        return (r * r,)

    (left,) = scan(second, 1)
    sums[...] = jnp.where(rows == 0, cross, jnp.where(rows == 1, square, left))


def apply_next(base, mine, packed, lefts, rights, sums, out):
    def block(t, k):
        other = [packed[t, k, n] for n in range(OPS // 2)]
        return jnp.concatenate(own_rows(mine, base[t, k]) + other, axis=0)

    products(block, lefts, rights, store_in(out))
    for i in range(OPS):
        out[i, SLOTS] = sums[...]


def finish_next(masks, parts, psi, sigma, next_vector, sigma_next):
    cross, square, left = [
        jnp.concatenate([parts[i, SLOTS, n : n + 1] for i in range(OPS)], axis=0) for n in range(3)
    ]
    theta = jnp.sum(cross, axis=0, keepdims=True) / jnp.sum(square, axis=0, keepdims=True)
    shift = projection(cross, square) - theta
    norm = jnp.sum(left + shift * square * shift, axis=0, keepdims=True)
    scale = 1.0 / jnp.sqrt(norm + 1e-06)
    for t in range(SLOTS):
        sigma_next[t] = (reduced(parts, t) * masks[t] - theta * sigma[t]) * scale
        next_vector[t] = (sigma[t] - theta * (psi[t] * masks[t])) * scale


def gather(copies):
    part = exchange(copies, FAR).reshape(1, CHUNKS // 8, ROWS, WIDTH)
    part = jnp.broadcast_to(part, (8, CHUNKS // 8, ROWS, WIDTH))
    return exchange(part, NEAR).reshape(CHUNKS, ROWS, WIDTH)


def on_device(psi, left_env, right_env, coupling, assign, sizes):
    ints = jnp.int32
    vec = shape(SLOTS, ROWS, WIDTH)
    chunk = shape(ROWS, WIDTH)
    parts_shape = shape(OPS, SLOTS + 1, ROWS, WIDTH)
    env_shape = shape(LOCAL_TERMS, SLOTS, WIDTH, 2 * WIDTH, dtype=BF16)
    flops = 2 * 2 * 32 * 128 * 256 * 256

    start_mine = gather(jnp.broadcast_to(psi[None], (SECS,) + psi.shape))
    start_other = lax.ppermute(start_mine, AXES, OTHER_CORE)
    base, bases, size_of, masks, lefts, rights = call(
        prepare,
        (
            shape(SLOTS, LOCAL_TERMS, dtype=ints),
            chunk,
            shape(SECTORS, dtype=ints),
            vec,
            env_shape,
            env_shape,
        ),
        (SMEM, VMEM, SMEM, VMEM, VMEM, VMEM),
        (HBM,) * 3 + (VMEM,) * 2,
        scratch=(
            pltpu.SMEM((SLOTS, LOCAL_TERMS), ints),
            pltpu.SMEM((SECTORS,), ints),
            pltpu.SMEM((SECTORS,), ints),
            pltpu.SMEM((SECTORS,), ints),
            pltpu.SemaphoreType.DMA((3,)),
        ),
        flops=flops,
        moved=8 << 20,
    )(coupling, assign, sizes, left_env, right_env)
    parts = call(apply_first, parts_shape, VMEM, (SMEM,) + (VMEM,) * 5, flops=flops)(
        base, bases, start_mine, start_other, lefts, rights
    )
    parts = exchange(parts, SAME_SEC)
    sigma_first, copies, other_base = call(
        finish_first,
        (vec, shape(SECS, SLOTS, ROWS, WIDTH), shape(ROWS, WIDTH, dtype=ints)),
        (VMEM,) * 3,
        (VMEM, VMEM),
    )(masks, parts)
    mine = gather(copies)
    packed = call(pack, shape(SLOTS, LOCAL_TERMS, OPS // 2, ROWS, WIDTH), VMEM, (SMEM, VMEM))(
        other_base, mine
    )
    other = lax.ppermute(packed, AXES, OTHER_CORE)
    sums = call(
        moments,
        chunk,
        VMEM,
        (SMEM, VMEM, VMEM),
        scratch=(pltpu.VMEM((SECTORS, ROWS, WIDTH), F32),),
        flops=flops,
    )(size_of, start_mine, mine)
    parts = call(apply_next, parts_shape, VMEM, (SMEM,) + (VMEM,) * 5, flops=flops)(
        base, mine, other, lefts, rights, sums
    )
    parts = exchange(parts, SAME_SEC)
    next_vector, sigma_next = call(finish_next, (vec, vec), (VMEM, VMEM), (VMEM,) * 4)(
        masks, parts, psi, sigma_first
    )
    return sigma_first, next_vector, sigma_next


def solution(mesh):
    placed = (
        P("sec", "op", None),
        P("op", "sec", None, None),
        P("op", "sec", None, None),
        P("sec", "op"),
        P(),
        P(),
    )
    return jax.shard_map(
        on_device,
        mesh=mesh,
        in_specs=placed,
        out_specs=(P("sec", "op", None),) * 3,
        check_vma=False,
    )
```

```python
import itertools

import jax
import jax.numpy as jnp
from jax import lax
from jax.experimental import pallas as pl
from jax.experimental.pallas import tpu as pltpu
from jax.sharding import PartitionSpec as P

AXES = ("op", "sec")
F32 = jnp.float32
BF16 = jnp.bfloat16
SLOTS, ROWS, WIDTH, LOCAL_TERMS = 2, 8, 128, 16
SECTORS = 64
OPS, SECS = 16, 32
CHUNKS = 512


PLACES = list(itertools.product(range(4), range(2), range(2), range(8), range(4)))


def number(x, zl, core, y, zh):
    return ((((x * 2 + zl) * 2 + core) * 8) + y) * 4 + zh


def groups(key, order):
    found = {}
    for place in PLACES:
        found.setdefault(key(*place), []).append((order(*place), number(*place)))
    return [[device for _, device in sorted(members)] for members in found.values()]


def cube(x, zl, core, y, zh):
    z = 2 * zh + zl
    return (x + core - 1) % 4 // 2, (y - core) % 8 // 2, (z - core) % 8 // 2, core


def kind(x, zl, core, y, zh):
    return (x + 2 * zl) % 4 * 2 + y % 2


SAME_SEC = groups(lambda x, zl, core, y, zh: (y, zh), lambda x, zl, core, y, zh: (x, zl, core))
FAR = groups(lambda *place: (kind(*place), place[2]), lambda x, zl, core, y, zh: (zh, zl, y // 2))
NEAR = groups(cube, kind)
OTHER_CORE = [
    (number(x, zl, core, y, zh), number(x, zl, 1 - core, y, zh)) for x, zl, core, y, zh in PLACES
]


def exchange(parts, members):
    return lax.all_to_all(parts, AXES, 0, 0, axis_index_groups=members)


VMEM = pl.BlockSpec(memory_space=pltpu.VMEM)
SMEM = pl.BlockSpec(memory_space=pltpu.SMEM)
HBM = pl.BlockSpec(memory_space=pltpu.HBM)


def call(body, outs, out_specs, in_specs, scratch=(), flops=0, moved=1 << 20):
    return pl.pallas_call(
        body,
        out_shape=outs,
        in_specs=in_specs,
        out_specs=out_specs,
        scratch_shapes=list(scratch),
        compiler_params=pltpu.CompilerParams(vmem_limit_bytes=40 << 20),
        cost_estimate=pl.CostEstimate(flops=flops, bytes_accessed=moved, transcendentals=0),
    )


def shape(*dims, dtype=F32):
    return jax.ShapeDtypeStruct(dims, dtype)


def inside(size, first_row):
    rows = first_row + lax.broadcasted_iota(jnp.int32, (ROWS, WIDTH), 0)
    cols = lax.broadcasted_iota(jnp.int32, (ROWS, WIDTH), 1)
    return (rows < size) & (cols < size)


def fetch(pairs, done):
    copies = [pltpu.make_async_copy(source, target, done.at[i]) for i, (source, target) in enumerate(pairs)]
    for copy in copies:
        copy.start()
    for copy in copies:
        copy.wait()


def halves(values):
    high = values.astype(BF16)
    return high, (values - high.astype(F32)).astype(BF16)


def prepare(
    coupling_hbm, assign_hbm, sizes_hbm, left, right, base, bases, size_of, masks, lefts, rights, coupling, assign, sizes, slot_of, done
):
    fetch([(coupling_hbm, coupling), (assign_hbm, assign), (sizes_hbm, sizes)], done)
    op = lax.axis_index("op")
    sub = lax.broadcasted_iota(jnp.int32, (ROWS, WIDTH), 0)
    lane = lax.broadcasted_iota(jnp.int32, (ROWS, WIDTH), 1)
    table = jnp.zeros((ROWS, WIDTH), jnp.int32)
    for p in range(SECTORS):
        sector = assign[p]
        slot_of[sector] = p
        size_of[p] = sizes[sector]
    for t in range(SLOTS):
        for k in range(LOCAL_TERMS):
            p = slot_of[coupling[t, k]]
            y = p // 8
            first = y % 2 * 64 + p % 8 // 2 * 16 + y // 2 * 2 + p % 2
            base[t, k] = first
            table = jnp.where((sub == t) & (lane == k), first, table)
        masks[t] = inside(size_of[lax.axis_index("sec") * SLOTS + t], op * ROWS).astype(F32)
    bases[...] = table.astype(F32)
    row = lax.broadcasted_iota(jnp.int32, (WIDTH, WIDTH), 0)
    col = lax.broadcasted_iota(jnp.int32, (WIDTH, WIDTH), 1)
    other = (row // 8 % 2 != op % 2).astype(jnp.int32)
    order = (col == other * 64 + row // 16 * 8 + row % 8).astype(F32).astype(BF16)
    for k in range(LOCAL_TERMS):
        for t in range(SLOTS):
            size = sizes[coupling[t, k]]
            high, low = halves(jnp.where(col < size, left[k, t], 0.0))
            moved = matmul(jnp.concatenate([high, low], axis=0), order).astype(BF16)
            lefts[k, t, :, :WIDTH] = moved[:WIDTH]
            lefts[k, t, :, WIDTH:] = moved[WIDTH:]
            high, low = halves(jnp.where(col < size, right[k, t], 0.0).T)
            rights[k, t, :, :WIDTH] = high
            rights[k, t, :, WIDTH:] = low


def matmul(a, b):
    return lax.dot_general(a, b, (((1,), (0,)), ((), ())), preferred_element_type=F32)


def products(block_of, lefts, rights, store):
    results = []
    for t in range(SLOTS):
        total = jnp.zeros((WIDTH, 2 * WIDTH), F32)
        for k in range(LOCAL_TERMS):
            high, low = halves(block_of(t, k))
            pair = jnp.concatenate([high, low], axis=1)
            inner = matmul(lefts[k, t], jnp.concatenate([pair, pair], axis=0))
            high, low = halves(inner[:, :WIDTH] + inner[:, WIDTH:])
            rows = rights[k, t]
            total = total + matmul(
                jnp.concatenate([high, low], axis=1), jnp.concatenate([rows, rows], axis=0)
            )
        results.append(total[:, :WIDTH] + total[:, WIDTH:])
    for t in range(SLOTS):
        for i in range(OPS):
            store(i, t, results[t][i * ROWS : (i + 1) * ROWS])


def own_rows(field, first):
    return [field[first + ((x + 2 * zl) % 4 * 128 + zl * 8)] for x in range(4) for zl in range(2)]


def gathered_block(mine, other, first):
    return jnp.concatenate(own_rows(mine, first) + own_rows(other, first), axis=0)


def store_in(out):
    def store(i, t, rows):
        out[i, t] = rows

    return store


def apply_first(base, bases, mine, other, lefts, rights, out):
    products(lambda t, k: gathered_block(mine, other, base[t, k]), lefts, rights, store_in(out))
    for i in range(OPS):
        out[i, SLOTS] = bases[...]


def reduced(parts, t):
    total = parts[0, t]
    for i in range(1, OPS):
        total = total + parts[i, t]
    return total


def finish_first(masks, parts, sigma, copies, other_base):
    op = lax.axis_index("op")
    for t in range(SLOTS):
        total = reduced(parts, t) * masks[t]
        sigma[t] = total
        for i in range(SECS):
            copies[i, t] = total
    other_base[...] = parts[op + 1 - 2 * (op % 2), SLOTS].astype(jnp.int32)


def pack(other_base, mine, packed):
    for t in range(SLOTS):
        for k in range(LOCAL_TERMS):
            for n, chunk in enumerate(own_rows(mine, other_base[t, k])):
                packed[t, k, n] = chunk


LANES = 4


def whole_sum(values):
    return jnp.sum(jnp.sum(values, axis=1, keepdims=True), axis=0, keepdims=True)


def scan(step, count):
    x, zl = lax.axis_index("op") // 4, lax.axis_index("op") // 2 % 2
    start = (x + 2 * zl) % 4 * 128 + zl * 8
    sums = [jnp.zeros((ROWS, WIDTH), F32)] * (count * LANES)
    for u, (yl, zh, yh, t) in enumerate(itertools.product(range(2), range(4), range(4), range(2))):
        for n, term in enumerate(step(u, (yl, zh, yh, t), start + (yl * 64 + zh * 16 + yh * 2 + t))):
            at = n * LANES + u % LANES
            sums[at] = sums[at] + term
    return [whole_sum(sum(sums[n : n + LANES])) for n in range(0, len(sums), LANES)]


def projection(cross, square):
    some = square > 0.0
    return jnp.where(some, cross / jnp.where(some, square, 1.0), 0.0)


def moments(size_of, start, field, sums, masked):
    op = lax.axis_index("op")
    rows = lax.broadcasted_iota(jnp.int32, (ROWS, WIDTH), 0)
    cols = lax.broadcasted_iota(jnp.int32, (ROWS, WIDTH), 1)

    def first(u, where, here):
        yl, zh, yh, t = where
        size = size_of[(yh * 2 + yl) * 8 + zh * 2 + t]
        s = jnp.where((cols < size) & (rows < size - op * ROWS), start[here], 0.0)
        masked[u] = s
        return s * field[here], s * s

    cross, square = scan(first, 2)
    theta = projection(cross, square)

    def second(u, where, here):
        r = field[here] - theta * masked[u]
        return (r * r,)

    (left,) = scan(second, 1)
    sums[...] = jnp.where(rows == 0, cross, jnp.where(rows == 1, square, left))


def apply_next(base, mine, packed, lefts, rights, sums, out):
    def block(t, k):
        other = [packed[t, k, n] for n in range(OPS // 2)]
        return jnp.concatenate(own_rows(mine, base[t, k]) + other, axis=0)

    products(block, lefts, rights, store_in(out))
    for i in range(OPS):
        out[i, SLOTS] = sums[...]


def finish_next(masks, parts, psi, sigma, next_vector, sigma_next):
    cross, square, left = [
        jnp.concatenate([parts[i, SLOTS, n : n + 1] for i in range(OPS)], axis=0) for n in range(3)
    ]
    theta = jnp.sum(cross, axis=0, keepdims=True) / jnp.sum(square, axis=0, keepdims=True)
    shift = projection(cross, square) - theta
    norm = jnp.sum(left + shift * square * shift, axis=0, keepdims=True)
    scale = 1.0 / jnp.sqrt(norm + 1e-06)
    for t in range(SLOTS):
        sigma_next[t] = (reduced(parts, t) * masks[t] - theta * sigma[t]) * scale
        next_vector[t] = (sigma[t] - theta * (psi[t] * masks[t])) * scale


def gather(copies):
    part = exchange(copies, FAR).reshape(1, CHUNKS // 8, ROWS, WIDTH)
    part = jnp.broadcast_to(part, (8, CHUNKS // 8, ROWS, WIDTH))
    return exchange(part, NEAR).reshape(CHUNKS, ROWS, WIDTH)


def on_device(psi, left_env, right_env, coupling, assign, sizes):
    ints = jnp.int32
    vec = shape(SLOTS, ROWS, WIDTH)
    chunk = shape(ROWS, WIDTH)
    parts_shape = shape(OPS, SLOTS + 1, ROWS, WIDTH)
    env_shape = shape(LOCAL_TERMS, SLOTS, WIDTH, 2 * WIDTH, dtype=BF16)
    flops = 2 * 2 * 32 * 128 * 256 * 256

    start_mine = gather(jnp.broadcast_to(psi[None], (SECS,) + psi.shape))
    start_other = lax.ppermute(start_mine, AXES, OTHER_CORE)
    base, bases, size_of, masks, lefts, rights = call(
        prepare,
        (
            shape(SLOTS, LOCAL_TERMS, dtype=ints),
            chunk,
            shape(SECTORS, dtype=ints),
            vec,
            env_shape,
            env_shape,
        ),
        (SMEM, VMEM, SMEM, VMEM, VMEM, VMEM),
        (HBM,) * 3 + (VMEM,) * 2,
        scratch=(
            pltpu.SMEM((SLOTS, LOCAL_TERMS), ints),
            pltpu.SMEM((SECTORS,), ints),
            pltpu.SMEM((SECTORS,), ints),
            pltpu.SMEM((SECTORS,), ints),
            pltpu.SemaphoreType.DMA((3,)),
        ),
        flops=flops,
        moved=8 << 20,
    )(coupling, assign, sizes, left_env, right_env)
    parts = call(apply_first, parts_shape, VMEM, (SMEM,) + (VMEM,) * 5, flops=flops)(
        base, bases, start_mine, start_other, lefts, rights
    )
    parts = exchange(parts, SAME_SEC)
    sigma_first, copies, other_base = call(
        finish_first,
        (vec, shape(SECS, SLOTS, ROWS, WIDTH), shape(ROWS, WIDTH, dtype=ints)),
        (VMEM,) * 3,
        (VMEM, VMEM),
    )(masks, parts)
    mine = gather(copies)
    packed = call(pack, shape(SLOTS, LOCAL_TERMS, OPS // 2, ROWS, WIDTH), VMEM, (SMEM, VMEM))(
        other_base, mine
    )
    other = lax.ppermute(packed, AXES, OTHER_CORE)
    sums = call(
        moments,
        chunk,
        VMEM,
        (SMEM, VMEM, VMEM),
        scratch=(pltpu.VMEM((SECTORS, ROWS, WIDTH), F32),),
        flops=flops,
    )(size_of, start_mine, mine)
    parts = call(apply_next, parts_shape, VMEM, (SMEM,) + (VMEM,) * 5, flops=flops)(
        base, mine, other, lefts, rights, sums
    )
    parts = exchange(parts, SAME_SEC)
    next_vector, sigma_next = call(finish_next, (vec, vec), (VMEM, VMEM), (VMEM,) * 4)(
        masks, parts, psi, sigma_first
    )
    return sigma_first, next_vector, sigma_next


def solution(mesh):
    placed = (
        P("sec", "op", None),
        P("op", "sec", None, None),
        P("op", "sec", None, None),
        P("sec", "op"),
        P(),
        P(),
    )
    return jax.shard_map(
        on_device,
        mesh=mesh,
        in_specs=placed,
        out_specs=(P("sec", "op", None),) * 3,
        check_vma=False,
    )
```

```python
import itertools

import jax
import jax.numpy as jnp
from jax import lax
from jax.experimental import pallas as pl
from jax.experimental.pallas import tpu as pltpu
from jax.sharding import PartitionSpec as P

AXES = ("op", "sec")
F32 = jnp.float32
BF16 = jnp.bfloat16
SLOTS, ROWS, WIDTH, LOCAL_TERMS = 2, 8, 128, 16
SECTORS = 64
OPS, SECS = 16, 32
CHUNKS = 512


PLACES = list(itertools.product(range(4), range(2), range(2), range(8), range(4)))


def number(x, zl, core, y, zh):
    return ((((x * 2 + zl) * 2 + core) * 8) + y) * 4 + zh


def groups(key, order):
    found = {}
    for place in PLACES:
        found.setdefault(key(*place), []).append((order(*place), number(*place)))
    return [[device for _, device in sorted(members)] for members in found.values()]


def cube(x, zl, core, y, zh):
    z = 2 * zh + zl
    return (x + core - 1) % 4 // 2, (y - core) % 8 // 2, (z - core) % 8 // 2, core


def kind(x, zl, core, y, zh):
    return (x + 2 * zl) % 4 * 2 + (y + zl) % 2


SAME_SEC = groups(lambda x, zl, core, y, zh: (y, zh), lambda x, zl, core, y, zh: (x, zl, core))
FAR = groups(lambda *place: (kind(*place), place[2]), lambda x, zl, core, y, zh: (zh, zl, y // 2))
NEAR = groups(cube, kind)
OTHER_CORE = [
    (number(x, zl, core, y, zh), number(x, zl, 1 - core, y, zh)) for x, zl, core, y, zh in PLACES
]


def exchange(parts, members):
    return lax.all_to_all(parts, AXES, 0, 0, axis_index_groups=members)


VMEM = pl.BlockSpec(memory_space=pltpu.VMEM)
SMEM = pl.BlockSpec(memory_space=pltpu.SMEM)
HBM = pl.BlockSpec(memory_space=pltpu.HBM)


def call(body, outs, out_specs, in_specs, scratch=(), flops=0, moved=1 << 20):
    return pl.pallas_call(
        body,
        out_shape=outs,
        in_specs=in_specs,
        out_specs=out_specs,
        scratch_shapes=list(scratch),
        compiler_params=pltpu.CompilerParams(vmem_limit_bytes=40 << 20),
        cost_estimate=pl.CostEstimate(flops=flops, bytes_accessed=moved, transcendentals=0),
    )


def shape(*dims, dtype=F32):
    return jax.ShapeDtypeStruct(dims, dtype)


def inside(size, first_row):
    rows = first_row + lax.broadcasted_iota(jnp.int32, (ROWS, WIDTH), 0)
    cols = lax.broadcasted_iota(jnp.int32, (ROWS, WIDTH), 1)
    return (rows < size) & (cols < size)


def fetch(pairs, done):
    copies = [pltpu.make_async_copy(source, target, done.at[i]) for i, (source, target) in enumerate(pairs)]
    for copy in copies:
        copy.start()
    for copy in copies:
        copy.wait()


def halves(values):
    high = values.astype(BF16)
    return high, (values - high.astype(F32)).astype(BF16)


def prepare(
    coupling_hbm, assign_hbm, sizes_hbm, left, right, base, bases, size_of, masks, lefts, rights, coupling, assign, sizes, slot_of, done
):
    fetch([(coupling_hbm, coupling), (assign_hbm, assign), (sizes_hbm, sizes)], done)
    op = lax.axis_index("op")
    sub = lax.broadcasted_iota(jnp.int32, (ROWS, WIDTH), 0)
    lane = lax.broadcasted_iota(jnp.int32, (ROWS, WIDTH), 1)
    table = jnp.zeros((ROWS, WIDTH), jnp.int32)
    for p in range(SECTORS):
        sector = assign[p]
        slot_of[sector] = p
        size_of[p] = sizes[sector]
    for t in range(SLOTS):
        for k in range(LOCAL_TERMS):
            p = slot_of[coupling[t, k]]
            y = p // 8
            first = y % 2 * 64 + p % 8 // 2 * 16 + y // 2 * 2 + p % 2
            base[t, k] = first
            table = jnp.where((sub == t) & (lane == k), first, table)
        masks[t] = inside(size_of[lax.axis_index("sec") * SLOTS + t], op * ROWS).astype(F32)
    bases[...] = table.astype(F32)
    row = lax.broadcasted_iota(jnp.int32, (WIDTH, WIDTH), 0)
    col = lax.broadcasted_iota(jnp.int32, (WIDTH, WIDTH), 1)
    other = (row // 8 % 2 != op % 2).astype(jnp.int32)
    order = (col == other * 64 + row // 16 * 8 + row % 8).astype(F32).astype(BF16)
    for k in range(LOCAL_TERMS):
        for t in range(SLOTS):
            size = sizes[coupling[t, k]]
            high, low = halves(jnp.where(col < size, left[k, t], 0.0))
            moved = matmul(jnp.concatenate([high, low], axis=0), order).astype(BF16)
            lefts[k, t, :, :WIDTH] = moved[:WIDTH]
            lefts[k, t, :, WIDTH:] = moved[WIDTH:]
            high, low = halves(jnp.where(col < size, right[k, t], 0.0).T)
            rights[k, t, :, :WIDTH] = high
            rights[k, t, :, WIDTH:] = low


def matmul(a, b):
    return lax.dot_general(a, b, (((1,), (0,)), ((), ())), preferred_element_type=F32)


def products(block_of, lefts, rights, store):
    results = []
    for t in range(SLOTS):
        total = jnp.zeros((WIDTH, 2 * WIDTH), F32)
        for k in range(LOCAL_TERMS):
            high, low = halves(block_of(t, k))
            pair = jnp.concatenate([high, low], axis=1)
            inner = matmul(lefts[k, t], jnp.concatenate([pair, pair], axis=0))
            high, low = halves(inner[:, :WIDTH] + inner[:, WIDTH:])
            rows = rights[k, t]
            total = total + matmul(
                jnp.concatenate([high, low], axis=1), jnp.concatenate([rows, rows], axis=0)
            )
        results.append(total[:, :WIDTH] + total[:, WIDTH:])
    for t in range(SLOTS):
        for i in range(OPS):
            store(i, t, results[t][i * ROWS : (i + 1) * ROWS])


def own_rows(field, first):
    starts = (first, first ^ 64)
    return [field[starts[zl] + ((x + 2 * zl) % 4 * 128 + zl * 8)] for x in range(4) for zl in range(2)]


def gathered_block(mine, other, first):
    return jnp.concatenate(own_rows(mine, first) + own_rows(other, first), axis=0)


def store_in(out):
    def store(i, t, rows):
        out[i, t] = rows

    return store


def apply_first(base, bases, mine, other, lefts, rights, out):
    products(lambda t, k: gathered_block(mine, other, base[t, k]), lefts, rights, store_in(out))
    for i in range(OPS):
        out[i, SLOTS] = bases[...]


def reduced(parts, t):
    total = parts[0, t]
    for i in range(1, OPS):
        total = total + parts[i, t]
    return total


def finish_first(masks, parts, sigma, copies, other_base):
    op = lax.axis_index("op")
    for t in range(SLOTS):
        total = reduced(parts, t) * masks[t]
        sigma[t] = total
        for i in range(SECS):
            copies[i, t] = total
    numbers = parts[op + 1 - 2 * (op % 2), SLOTS]
    other_base[...] = numbers[:SLOTS, :LOCAL_TERMS].astype(jnp.int32)


def pack(other_base, mine, packed):
    for t in range(SLOTS):
        for k in range(LOCAL_TERMS):
            for n, chunk in enumerate(own_rows(mine, other_base[t, k])):
                packed[t, k, n] = chunk


LANES = 4


def whole_sum(values):
    return jnp.sum(jnp.sum(values, axis=1, keepdims=True), axis=0, keepdims=True)


def scan(step, count):
    x, zl = lax.axis_index("op") // 4, lax.axis_index("op") // 2 % 2
    start = (x + 2 * zl) % 4 * 128 + zl * 8
    sums = [jnp.zeros((ROWS, WIDTH), F32)] * (count * LANES)
    for u, (yl, zh, yh, t) in enumerate(itertools.product(range(2), range(4), range(4), range(2))):
        for n, term in enumerate(step(u, (yl, zh, yh, t), start + (yl * 64 + zh * 16 + yh * 2 + t))):
            at = n * LANES + u % LANES
            sums[at] = sums[at] + term
    return [whole_sum(sum(sums[n : n + LANES])) for n in range(0, len(sums), LANES)]


def projection(cross, square):
    some = square > 0.0
    return jnp.where(some, cross / jnp.where(some, square, 1.0), 0.0)


def moments(size_of, start, field, sums, masked):
    op = lax.axis_index("op")
    rows = lax.broadcasted_iota(jnp.int32, (ROWS, WIDTH), 0)
    cols = lax.broadcasted_iota(jnp.int32, (ROWS, WIDTH), 1)

    def first(u, where, here):
        yl, zh, yh, t = where
        y = yh * 2 + (yl + op // 2) % 2
        size = size_of[y * 8 + zh * 2 + t]
        s = jnp.where((cols < size) & (rows < size - op * ROWS), start[here], 0.0)
        masked[u] = s
        return s * field[here], s * s

    cross, square = scan(first, 2)
    theta = projection(cross, square)

    def second(u, where, here):
        r = field[here] - theta * masked[u]
        return (r * r,)

    (left,) = scan(second, 1)
    sums[...] = jnp.where(rows == 0, cross, jnp.where(rows == 1, square, left))


def apply_next(base, mine, packed, lefts, rights, sums, out):
    def block(t, k):
        other = [packed[t, k, n] for n in range(OPS // 2)]
        return jnp.concatenate(own_rows(mine, base[t, k]) + other, axis=0)

    products(block, lefts, rights, store_in(out))
    for i in range(OPS):
        out[i, SLOTS] = sums[...]


def finish_next(masks, parts, psi, sigma, next_vector, sigma_next):
    cross, square, left = [
        jnp.concatenate([parts[i, SLOTS, n : n + 1] for i in range(OPS)], axis=0) for n in range(3)
    ]
    theta = jnp.sum(cross, axis=0, keepdims=True) / jnp.sum(square, axis=0, keepdims=True)
    shift = projection(cross, square) - theta
    norm = jnp.sum(left + shift * square * shift, axis=0, keepdims=True)
    scale = 1.0 / jnp.sqrt(norm + 1e-06)
    for t in range(SLOTS):
        sigma_next[t] = (reduced(parts, t) * masks[t] - theta * sigma[t]) * scale
        next_vector[t] = (sigma[t] - theta * (psi[t] * masks[t])) * scale


def gather(copies):
    part = exchange(copies, FAR).reshape(1, CHUNKS // 8, ROWS, WIDTH)
    part = jnp.broadcast_to(part, (8, CHUNKS // 8, ROWS, WIDTH))
    return exchange(part, NEAR).reshape(CHUNKS, ROWS, WIDTH)


def on_device(psi, left_env, right_env, coupling, assign, sizes):
    ints = jnp.int32
    vec = shape(SLOTS, ROWS, WIDTH)
    chunk = shape(ROWS, WIDTH)
    parts_shape = shape(OPS, SLOTS + 1, ROWS, WIDTH)
    env_shape = shape(LOCAL_TERMS, SLOTS, WIDTH, 2 * WIDTH, dtype=BF16)
    flops = 2 * 2 * 32 * 128 * 256 * 256

    start_mine = gather(jnp.broadcast_to(psi[None], (SECS,) + psi.shape))
    start_other = lax.ppermute(start_mine, AXES, OTHER_CORE)
    base, bases, size_of, masks, lefts, rights = call(
        prepare,
        (
            shape(SLOTS, LOCAL_TERMS, dtype=ints),
            chunk,
            shape(SECTORS, dtype=ints),
            vec,
            env_shape,
            env_shape,
        ),
        (SMEM, VMEM, SMEM, VMEM, VMEM, VMEM),
        (HBM,) * 3 + (VMEM,) * 2,
        scratch=(
            pltpu.SMEM((SLOTS, LOCAL_TERMS), ints),
            pltpu.SMEM((SECTORS,), ints),
            pltpu.SMEM((SECTORS,), ints),
            pltpu.SMEM((SECTORS,), ints),
            pltpu.SemaphoreType.DMA((3,)),
        ),
        flops=flops,
        moved=8 << 20,
    )(coupling, assign, sizes, left_env, right_env)
    parts = call(apply_first, parts_shape, VMEM, (SMEM,) + (VMEM,) * 5, flops=flops)(
        base, bases, start_mine, start_other, lefts, rights
    )
    parts = exchange(parts, SAME_SEC)
    sigma_first, copies, other_base = call(
        finish_first,
        (vec, shape(SECS, SLOTS, ROWS, WIDTH), shape(SLOTS, LOCAL_TERMS, dtype=ints)),
        (VMEM,) * 3,
        (VMEM, VMEM),
    )(masks, parts)
    mine = gather(copies)
    packed = call(pack, shape(SLOTS, LOCAL_TERMS, OPS // 2, ROWS, WIDTH), VMEM, (SMEM, VMEM))(
        other_base, mine
    )
    other = lax.ppermute(packed, AXES, OTHER_CORE)
    sums = call(
        moments,
        chunk,
        VMEM,
        (SMEM, VMEM, VMEM),
        scratch=(pltpu.VMEM((SECTORS, ROWS, WIDTH), F32),),
        flops=flops,
    )(size_of, start_mine, mine)
    parts = call(apply_next, parts_shape, VMEM, (SMEM,) + (VMEM,) * 5, flops=flops)(
        base, mine, other, lefts, rights, sums
    )
    parts = exchange(parts, SAME_SEC)
    next_vector, sigma_next = call(finish_next, (vec, vec), (VMEM, VMEM), (VMEM,) * 4)(
        masks, parts, psi, sigma_first
    )
    return sigma_first, next_vector, sigma_next


def solution(mesh):
    placed = (
        P("sec", "op", None),
        P("op", "sec", None, None),
        P("op", "sec", None, None),
        P("sec", "op"),
        P(),
        P(),
    )
    return jax.shard_map(
        on_device,
        mesh=mesh,
        in_specs=placed,
        out_specs=(P("sec", "op", None),) * 3,
        check_vma=False,
    )
```

```python
import itertools

import jax
import jax.numpy as jnp
from jax import lax
from jax.experimental import pallas as pl
from jax.experimental.pallas import tpu as pltpu
from jax.sharding import PartitionSpec as P

AXES = ("op", "sec")
F32 = jnp.float32
BF16 = jnp.bfloat16
SLOTS, ROWS, WIDTH, LOCAL_TERMS = 2, 8, 128, 16
SECTORS = 64
OPS, SECS = 16, 32
CHUNKS = 512


PLACES = list(itertools.product(range(4), range(2), range(2), range(8), range(4)))


def number(x, zl, core, y, zh):
    return ((((x * 2 + zl) * 2 + core) * 8) + y) * 4 + zh


def groups(key, order):
    found = {}
    for place in PLACES:
        found.setdefault(key(*place), []).append((order(*place), number(*place)))
    return [[device for _, device in sorted(members)] for members in found.values()]


def cube(x, zl, core, y, zh):
    z = 2 * zh + zl
    return (x + core - 1) % 4 // 2, (y - core) % 8 // 2, (z - core) % 8 // 2, core


def kind(x, zl, core, y, zh):
    return (x + 2 * zl) % 4 * 2 + (y + zl) % 2


SAME_SEC = groups(lambda x, zl, core, y, zh: (y, zh), lambda x, zl, core, y, zh: (x, zl, core))
FAR = groups(lambda *place: (kind(*place), place[2]), lambda x, zl, core, y, zh: (zh, zl, y // 2))
NEAR = groups(cube, kind)
OTHER_CORE = [
    (number(x, zl, core, y, zh), number(x, zl, 1 - core, y, zh)) for x, zl, core, y, zh in PLACES
]


def exchange(parts, members):
    return lax.all_to_all(parts, AXES, 0, 0, axis_index_groups=members)


VMEM = pl.BlockSpec(memory_space=pltpu.VMEM)
SMEM = pl.BlockSpec(memory_space=pltpu.SMEM)
HBM = pl.BlockSpec(memory_space=pltpu.HBM)


def call(body, outs, out_specs, in_specs, scratch=(), flops=0, moved=1 << 20):
    return pl.pallas_call(
        body,
        out_shape=outs,
        in_specs=in_specs,
        out_specs=out_specs,
        scratch_shapes=list(scratch),
        compiler_params=pltpu.CompilerParams(vmem_limit_bytes=40 << 20),
        cost_estimate=pl.CostEstimate(flops=flops, bytes_accessed=moved, transcendentals=0),
    )


def shape(*dims, dtype=F32):
    return jax.ShapeDtypeStruct(dims, dtype)


def inside(size, first_row):
    rows = first_row + lax.broadcasted_iota(jnp.int32, (ROWS, WIDTH), 0)
    cols = lax.broadcasted_iota(jnp.int32, (ROWS, WIDTH), 1)
    return (rows < size) & (cols < size)


def fetch(pairs, done):
    copies = [pltpu.make_async_copy(source, target, done.at[i]) for i, (source, target) in enumerate(pairs)]
    for copy in copies:
        copy.start()
    for copy in copies:
        copy.wait()


def halves(values):
    high = values.astype(BF16)
    return high, (values - high.astype(F32)).astype(BF16)


def prepare(
    coupling_hbm, assign_hbm, sizes_hbm, left, right, base, bases, size_of, masks, lefts, rights, coupling, assign, sizes, slot_of, done
):
    fetch([(coupling_hbm, coupling), (assign_hbm, assign), (sizes_hbm, sizes)], done)
    op = lax.axis_index("op")
    sub = lax.broadcasted_iota(jnp.int32, (ROWS, WIDTH), 0)
    lane = lax.broadcasted_iota(jnp.int32, (ROWS, WIDTH), 1)
    table = jnp.zeros((ROWS, WIDTH), jnp.int32)
    for p in range(SECTORS):
        sector = assign[p]
        slot_of[sector] = p
        size_of[p] = sizes[sector]
    for t in range(SLOTS):
        for k in range(LOCAL_TERMS):
            p = slot_of[coupling[t, k]]
            y = p // 8
            first = y % 2 * 64 + p % 8 // 2 * 16 + y // 2 * 2 + p % 2
            base[t, k] = first
            table = jnp.where((sub == t) & (lane == k), first, table)
        masks[t] = inside(size_of[lax.axis_index("sec") * SLOTS + t], op * ROWS).astype(F32)
    bases[...] = table.astype(F32)
    row = lax.broadcasted_iota(jnp.int32, (WIDTH, WIDTH), 0)
    col = lax.broadcasted_iota(jnp.int32, (WIDTH, WIDTH), 1)
    other = (row // 8 % 2 != op % 2).astype(jnp.int32)
    spot = other * 128 + row // 16 * 8 + row % 8
    lanes = lax.broadcasted_iota(jnp.int32, (WIDTH, 2 * WIDTH), 1)
    spots = jnp.concatenate([spot, spot], axis=1)
    order = jnp.concatenate([lanes == spots, lanes == spots + 64], axis=0).astype(F32).astype(BF16)
    for k in range(LOCAL_TERMS):
        for t in range(SLOTS):
            size = sizes[coupling[t, k]]
            high, low = halves(jnp.where(col < size, left[k, t], 0.0))
            lefts[k, t] = matmul(jnp.concatenate([high, low], axis=1), order).astype(BF16)
            high, low = halves(jnp.where(col < size, right[k, t], 0.0).T)
            rights[k, t, :, :WIDTH] = high
            rights[k, t, :, WIDTH:] = low


def matmul(a, b):
    return lax.dot_general(a, b, (((1,), (0,)), ((), ())), preferred_element_type=F32)


def part_product(columns, chunks):
    high, low = halves(jnp.concatenate(chunks, axis=0))
    pair = jnp.concatenate([high, low], axis=1)
    result = matmul(columns, jnp.concatenate([pair, pair], axis=0))
    return result[:, :WIDTH] + result[:, WIDTH:]


def own_products(base, mine, lefts, inner):
    for t in range(SLOTS):
        for k in range(LOCAL_TERMS):
            inner[t, k] = part_product(lefts[k, t, :, :WIDTH], own_rows(mine, base[t, k]))


def products(other_rows, inner, lefts, rights, out):
    for t in range(SLOTS):
        total = jnp.zeros((WIDTH, 2 * WIDTH), F32)
        for k in range(LOCAL_TERMS):
            high, low = halves(inner[t, k] + part_product(lefts[k, t, :, WIDTH:], other_rows(t, k)))
            rows = rights[k, t]
            total = total + matmul(
                jnp.concatenate([high, low], axis=1), jnp.concatenate([rows, rows], axis=0)
            )
        result = total[:, :WIDTH] + total[:, WIDTH:]
        for i in range(OPS):
            out[i, t] = result[i * ROWS : (i + 1) * ROWS]


def own_rows(field, first):
    starts = (first, first ^ 64)
    return [field[starts[zl] + ((x + 2 * zl) % 4 * 128 + zl * 8)] for x in range(4) for zl in range(2)]


def apply_first(base, bases, inner, other, lefts, rights, out):
    products(lambda t, k: own_rows(other, base[t, k]), inner, lefts, rights, out)
    for i in range(OPS):
        out[i, SLOTS] = bases[...]


def reduced(parts, t):
    total = parts[0, t]
    for i in range(1, OPS):
        total = total + parts[i, t]
    return total


def finish_first(masks, parts, sigma, copies, other_base):
    op = lax.axis_index("op")
    for t in range(SLOTS):
        total = reduced(parts, t) * masks[t]
        sigma[t] = total
        for i in range(SECS):
            copies[i, t] = total
    numbers = parts[op + 1 - 2 * (op % 2), SLOTS]
    other_base[...] = numbers[:SLOTS, :LOCAL_TERMS].astype(jnp.int32)


def pack(other_base, mine, packed):
    for t in range(SLOTS):
        for k in range(LOCAL_TERMS):
            for n, chunk in enumerate(own_rows(mine, other_base[t, k])):
                packed[t, k, n] = chunk


LANES = 4


def whole_sum(values):
    return jnp.sum(jnp.sum(values, axis=1, keepdims=True), axis=0, keepdims=True)


def scan(step, count):
    x, zl = lax.axis_index("op") // 4, lax.axis_index("op") // 2 % 2
    start = (x + 2 * zl) % 4 * 128 + zl * 8
    sums = [jnp.zeros((ROWS, WIDTH), F32)] * (count * LANES)
    for u, (yl, zh, yh, t) in enumerate(itertools.product(range(2), range(4), range(4), range(2))):
        for n, term in enumerate(step(u, (yl, zh, yh, t), start + (yl * 64 + zh * 16 + yh * 2 + t))):
            at = n * LANES + u % LANES
            sums[at] = sums[at] + term
    return [whole_sum(sum(sums[n : n + LANES])) for n in range(0, len(sums), LANES)]


def projection(cross, square):
    some = square > 0.0
    return jnp.where(some, cross / jnp.where(some, square, 1.0), 0.0)


def moments(size_of, start, field, sums, masked):
    op = lax.axis_index("op")
    rows = lax.broadcasted_iota(jnp.int32, (ROWS, WIDTH), 0)
    cols = lax.broadcasted_iota(jnp.int32, (ROWS, WIDTH), 1)

    def first(u, where, here):
        yl, zh, yh, t = where
        y = yh * 2 + (yl + op // 2) % 2
        size = size_of[y * 8 + zh * 2 + t]
        s = jnp.where((cols < size) & (rows < size - op * ROWS), start[here], 0.0)
        masked[u] = s
        return s * field[here], s * s

    cross, square = scan(first, 2)
    theta = projection(cross, square)

    def second(u, where, here):
        r = field[here] - theta * masked[u]
        return (r * r,)

    (left,) = scan(second, 1)
    sums[...] = jnp.where(rows == 0, cross, jnp.where(rows == 1, square, left))


def apply_next(inner, packed, lefts, rights, sums, out):
    products(lambda t, k: [packed[t, k, n] for n in range(OPS // 2)], inner, lefts, rights, out)
    for i in range(OPS):
        out[i, SLOTS] = sums[...]


def finish_next(masks, parts, psi, sigma, next_vector, sigma_next):
    cross, square, left = [
        jnp.concatenate([parts[i, SLOTS, n : n + 1] for i in range(OPS)], axis=0) for n in range(3)
    ]
    theta = jnp.sum(cross, axis=0, keepdims=True) / jnp.sum(square, axis=0, keepdims=True)
    shift = projection(cross, square) - theta
    norm = jnp.sum(left + shift * square * shift, axis=0, keepdims=True)
    scale = 1.0 / jnp.sqrt(norm + 1e-06)
    for t in range(SLOTS):
        sigma_next[t] = (reduced(parts, t) * masks[t] - theta * sigma[t]) * scale
        next_vector[t] = (sigma[t] - theta * (psi[t] * masks[t])) * scale


def gather(copies):
    part = exchange(copies, FAR).reshape(1, CHUNKS // 8, ROWS, WIDTH)
    part = jnp.broadcast_to(part, (8, CHUNKS // 8, ROWS, WIDTH))
    return exchange(part, NEAR).reshape(CHUNKS, ROWS, WIDTH)


def on_device(psi, left_env, right_env, coupling, assign, sizes):
    ints = jnp.int32
    vec = shape(SLOTS, ROWS, WIDTH)
    chunk = shape(ROWS, WIDTH)
    parts_shape = shape(OPS, SLOTS + 1, ROWS, WIDTH)
    env_shape = shape(LOCAL_TERMS, SLOTS, WIDTH, 2 * WIDTH, dtype=BF16)
    flops = 2 * 2 * 32 * 128 * 256 * 256

    start_mine = gather(jnp.broadcast_to(psi[None], (SECS,) + psi.shape))
    start_other = lax.ppermute(start_mine, AXES, OTHER_CORE)
    base, bases, size_of, masks, lefts, rights = call(
        prepare,
        (
            shape(SLOTS, LOCAL_TERMS, dtype=ints),
            chunk,
            shape(SECTORS, dtype=ints),
            vec,
            env_shape,
            env_shape,
        ),
        (SMEM, VMEM, SMEM, VMEM, VMEM, VMEM),
        (HBM,) * 3 + (VMEM,) * 2,
        scratch=(
            pltpu.SMEM((SLOTS, LOCAL_TERMS), ints),
            pltpu.SMEM((SECTORS,), ints),
            pltpu.SMEM((SECTORS,), ints),
            pltpu.SMEM((SECTORS,), ints),
            pltpu.SemaphoreType.DMA((3,)),
        ),
        flops=flops,
        moved=8 << 20,
    )(coupling, assign, sizes, left_env, right_env)
    inner_shape = shape(SLOTS, LOCAL_TERMS, WIDTH, WIDTH)
    own = call(own_products, inner_shape, VMEM, (SMEM, VMEM, VMEM), flops=flops // 2)
    parts = call(apply_first, parts_shape, VMEM, (SMEM,) + (VMEM,) * 5, flops=flops)(
        base, bases, own(base, start_mine, lefts), start_other, lefts, rights
    )
    parts = exchange(parts, SAME_SEC)
    sigma_first, copies, other_base = call(
        finish_first,
        (vec, shape(SECS, SLOTS, ROWS, WIDTH), shape(SLOTS, LOCAL_TERMS, dtype=ints)),
        (VMEM,) * 3,
        (VMEM, VMEM),
    )(masks, parts)
    mine = gather(copies)
    packed = call(pack, shape(SLOTS, LOCAL_TERMS, OPS // 2, ROWS, WIDTH), VMEM, (SMEM, VMEM))(
        other_base, mine
    )
    other = lax.ppermute(packed, AXES, OTHER_CORE)
    sums = call(
        moments,
        chunk,
        VMEM,
        (SMEM, VMEM, VMEM),
        scratch=(pltpu.VMEM((SECTORS, ROWS, WIDTH), F32),),
        flops=flops,
    )(size_of, start_mine, mine)
    parts = call(apply_next, parts_shape, VMEM, (VMEM,) * 5, flops=flops)(
        own(base, mine, lefts), other, lefts, rights, sums
    )
    parts = exchange(parts, SAME_SEC)
    next_vector, sigma_next = call(finish_next, (vec, vec), (VMEM, VMEM), (VMEM,) * 4)(
        masks, parts, psi, sigma_first
    )
    return sigma_first, next_vector, sigma_next


def solution(mesh):
    placed = (
        P("sec", "op", None),
        P("op", "sec", None, None),
        P("op", "sec", None, None),
        P("sec", "op"),
        P(),
        P(),
    )
    return jax.shard_map(
        on_device,
        mesh=mesh,
        in_specs=placed,
        out_specs=(P("sec", "op", None),) * 3,
        check_vma=False,
    )
```

```python
import itertools

import jax
import jax.numpy as jnp
from jax import lax
from jax.experimental import pallas as pl
from jax.experimental.pallas import tpu as pltpu
from jax.sharding import PartitionSpec as P

AXES = ("op", "sec")
F32 = jnp.float32
BF16 = jnp.bfloat16
SLOTS, ROWS, WIDTH, LOCAL_TERMS = 2, 8, 128, 16
SECTORS = 64
OPS, SECS = 16, 32
CHUNKS = 512


PLACES = list(itertools.product(range(4), range(2), range(2), range(8), range(4)))


def number(x, zl, core, y, zh):
    return ((((x * 2 + zl) * 2 + core) * 8) + y) * 4 + zh


def groups(key, order):
    found = {}
    for place in PLACES:
        found.setdefault(key(*place), []).append((order(*place), number(*place)))
    return [[device for _, device in sorted(members)] for members in found.values()]


def cube(x, zl, core, y, zh):
    z = 2 * zh + zl
    return (x + core - 1) % 4 // 2, (y - core) % 8 // 2, (z - core) % 8 // 2, core


def kind(x, zl, core, y, zh):
    return (x + 2 * zl) % 4 * 2 + (y + zl) % 2


SAME_SEC = groups(lambda x, zl, core, y, zh: (y, zh), lambda x, zl, core, y, zh: (x, zl, core))
FAR = groups(lambda *place: (kind(*place), place[2]), lambda x, zl, core, y, zh: (zh, zl, y // 2))
NEAR = groups(cube, kind)
OTHER_CORE = [
    (number(x, zl, core, y, zh), number(x, zl, 1 - core, y, zh)) for x, zl, core, y, zh in PLACES
]


def exchange(parts, members):
    return lax.all_to_all(parts, AXES, 0, 0, axis_index_groups=members)


VMEM = pl.BlockSpec(memory_space=pltpu.VMEM)
SMEM = pl.BlockSpec(memory_space=pltpu.SMEM)
HBM = pl.BlockSpec(memory_space=pltpu.HBM)


def call(body, outs, out_specs, in_specs, scratch=(), flops=0, moved=1 << 20):
    return pl.pallas_call(
        body,
        out_shape=outs,
        in_specs=in_specs,
        out_specs=out_specs,
        scratch_shapes=list(scratch),
        compiler_params=pltpu.CompilerParams(vmem_limit_bytes=40 << 20),
        cost_estimate=pl.CostEstimate(flops=flops, bytes_accessed=moved, transcendentals=0),
    )


def shape(*dims, dtype=F32):
    return jax.ShapeDtypeStruct(dims, dtype)


def inside(size, first_row):
    rows = first_row + lax.broadcasted_iota(jnp.int32, (ROWS, WIDTH), 0)
    cols = lax.broadcasted_iota(jnp.int32, (ROWS, WIDTH), 1)
    return (rows < size) & (cols < size)


def fetch(pairs, done):
    copies = [pltpu.make_async_copy(source, target, done.at[i]) for i, (source, target) in enumerate(pairs)]
    for copy in copies:
        copy.start()
    for copy in copies:
        copy.wait()


def halves(values):
    high = values.astype(BF16)
    return high, (values - high.astype(F32)).astype(BF16)


def prepare(
    coupling_hbm, assign_hbm, sizes_hbm, left, right, base, bases, size_of, masks, lefts, rights, coupling, assign, sizes, slot_of, done
):
    fetch([(coupling_hbm, coupling), (assign_hbm, assign), (sizes_hbm, sizes)], done)
    op = lax.axis_index("op")
    sub = lax.broadcasted_iota(jnp.int32, (ROWS, WIDTH), 0)
    lane = lax.broadcasted_iota(jnp.int32, (ROWS, WIDTH), 1)
    table = jnp.zeros((ROWS, WIDTH), jnp.int32)
    for p in range(SECTORS):
        sector = assign[p]
        slot_of[sector] = p
        size_of[p] = sizes[sector]
    for t in range(SLOTS):
        for k in range(LOCAL_TERMS):
            p = slot_of[coupling[t, k]]
            y = p // 8
            first = y % 2 * 64 + p % 8 // 2 * 16 + y // 2 * 2 + p % 2
            base[t, k] = first
            table = jnp.where((sub == t) & (lane == k), first, table)
        masks[t] = inside(size_of[lax.axis_index("sec") * SLOTS + t], op * ROWS).astype(F32)
    bases[...] = table.astype(F32)
    row = lax.broadcasted_iota(jnp.int32, (WIDTH, WIDTH), 0)
    col = lax.broadcasted_iota(jnp.int32, (WIDTH, WIDTH), 1)
    other = (row // 8 % 2 != op % 2).astype(jnp.int32)
    spot = other * 128 + row // 16 * 8 + row % 8
    lanes = lax.broadcasted_iota(jnp.int32, (WIDTH, 2 * WIDTH), 1)
    spots = jnp.concatenate([spot, spot], axis=1)
    order = jnp.concatenate([lanes == spots, lanes == spots + 64], axis=0).astype(F32).astype(BF16)
    for k in range(LOCAL_TERMS):
        for t in range(SLOTS):
            size = sizes[coupling[t, k]]
            high, low = halves(jnp.where(col < size, left[k, t], 0.0))
            lefts[k, t] = matmul(jnp.concatenate([high, low], axis=1), order).astype(BF16)
            high, low = halves(jnp.where(col < size, right[k, t], 0.0).T)
            rights[k, t, :, :WIDTH] = high
            rights[k, t, :, WIDTH:] = low


def matmul(a, b):
    return lax.dot_general(a, b, (((1,), (0,)), ((), ())), preferred_element_type=F32)


def part_product(columns, chunks):
    high, low = halves(jnp.concatenate(chunks, axis=0))
    pair = jnp.concatenate([high, low], axis=1)
    result = matmul(columns, jnp.concatenate([pair, pair], axis=0))
    return result[:, :WIDTH] + result[:, WIDTH:]


def own_products(base, mine, lefts, inner):
    for t in range(SLOTS):
        for k in range(LOCAL_TERMS):
            inner[t, k] = part_product(lefts[k, t, :, :WIDTH], own_rows(mine, base[t, k]))


def products(inner, rights, out):
    for t in range(SLOTS):
        total = jnp.zeros((WIDTH, 2 * WIDTH), F32)
        for k in range(LOCAL_TERMS):
            high, low = halves(inner(t, k))
            rows = rights[k, t]
            total = total + matmul(
                jnp.concatenate([high, low], axis=1), jnp.concatenate([rows, rows], axis=0)
            )
        result = total[:, :WIDTH] + total[:, WIDTH:]
        for i in range(OPS):
            out[i, t] = result[i * ROWS : (i + 1) * ROWS]


def own_rows(field, first):
    starts = (first, first ^ 64)
    return [field[starts[zl] + ((x + 2 * zl) % 4 * 128 + zl * 8)] for x in range(4) for zl in range(2)]


def apply_first(base, bases, mine, other, lefts, rights, out):
    def inner(t, k):
        pairs = []
        for field in (mine, other):
            high, low = halves(jnp.concatenate(own_rows(field, base[t, k]), axis=0))
            pairs += [jnp.concatenate([high, low], axis=1)] * 2
        result = matmul(lefts[k, t], jnp.concatenate(pairs, axis=0))
        return result[:, :WIDTH] + result[:, WIDTH:]

    products(inner, rights, out)
    for i in range(OPS):
        out[i, SLOTS] = bases[...]


def reduced(parts, t):
    total = parts[0, t]
    for i in range(1, OPS):
        total = total + parts[i, t]
    return total


def finish_first(masks, parts, sigma, copies, other_base):
    op = lax.axis_index("op")
    for t in range(SLOTS):
        total = reduced(parts, t) * masks[t]
        sigma[t] = total
        for i in range(SECS):
            copies[i, t] = total
    numbers = parts[op + 1 - 2 * (op % 2), SLOTS]
    other_base[...] = numbers[:SLOTS, :LOCAL_TERMS].astype(jnp.int32)


def pack(other_base, mine, packed):
    for t in range(SLOTS):
        for k in range(LOCAL_TERMS):
            for n, chunk in enumerate(own_rows(mine, other_base[t, k])):
                packed[t, k, n] = chunk


LANES = 4


def whole_sum(values):
    return jnp.sum(jnp.sum(values, axis=1, keepdims=True), axis=0, keepdims=True)


def scan(step, count):
    x, zl = lax.axis_index("op") // 4, lax.axis_index("op") // 2 % 2
    start = (x + 2 * zl) % 4 * 128 + zl * 8
    sums = [jnp.zeros((ROWS, WIDTH), F32)] * (count * LANES)
    for u, (yl, zh, yh, t) in enumerate(itertools.product(range(2), range(4), range(4), range(2))):
        for n, term in enumerate(step(u, (yl, zh, yh, t), start + (yl * 64 + zh * 16 + yh * 2 + t))):
            at = n * LANES + u % LANES
            sums[at] = sums[at] + term
    return [whole_sum(sum(sums[n : n + LANES])) for n in range(0, len(sums), LANES)]


def projection(cross, square):
    some = square > 0.0
    return jnp.where(some, cross / jnp.where(some, square, 1.0), 0.0)


def moments(size_of, start, field, sums, masked):
    op = lax.axis_index("op")
    rows = lax.broadcasted_iota(jnp.int32, (ROWS, WIDTH), 0)
    cols = lax.broadcasted_iota(jnp.int32, (ROWS, WIDTH), 1)

    def first(u, where, here):
        yl, zh, yh, t = where
        y = yh * 2 + (yl + op // 2) % 2
        size = size_of[y * 8 + zh * 2 + t]
        s = jnp.where((cols < size) & (rows < size - op * ROWS), start[here], 0.0)
        masked[u] = s
        return s * field[here], s * s

    cross, square = scan(first, 2)
    theta = projection(cross, square)

    def second(u, where, here):
        r = field[here] - theta * masked[u]
        return (r * r,)

    (left,) = scan(second, 1)
    sums[...] = jnp.where(rows == 0, cross, jnp.where(rows == 1, square, left))


def apply_next(own, packed, lefts, rights, sums, out):
    def inner(t, k):
        other = [packed[t, k, n] for n in range(OPS // 2)]
        return own[t, k] + part_product(lefts[k, t, :, WIDTH:], other)

    products(inner, rights, out)
    for i in range(OPS):
        out[i, SLOTS] = sums[...]


def finish_next(masks, parts, psi, sigma, next_vector, sigma_next):
    cross, square, left = [
        jnp.concatenate([parts[i, SLOTS, n : n + 1] for i in range(OPS)], axis=0) for n in range(3)
    ]
    theta = jnp.sum(cross, axis=0, keepdims=True) / jnp.sum(square, axis=0, keepdims=True)
    shift = projection(cross, square) - theta
    norm = jnp.sum(left + shift * square * shift, axis=0, keepdims=True)
    scale = 1.0 / jnp.sqrt(norm + 1e-06)
    for t in range(SLOTS):
        sigma_next[t] = (reduced(parts, t) * masks[t] - theta * sigma[t]) * scale
        next_vector[t] = (sigma[t] - theta * (psi[t] * masks[t])) * scale


def gather(copies):
    part = exchange(copies, FAR).reshape(1, CHUNKS // 8, ROWS, WIDTH)
    part = jnp.broadcast_to(part, (8, CHUNKS // 8, ROWS, WIDTH))
    return exchange(part, NEAR).reshape(CHUNKS, ROWS, WIDTH)


def on_device(psi, left_env, right_env, coupling, assign, sizes):
    ints = jnp.int32
    vec = shape(SLOTS, ROWS, WIDTH)
    chunk = shape(ROWS, WIDTH)
    parts_shape = shape(OPS, SLOTS + 1, ROWS, WIDTH)
    env_shape = shape(LOCAL_TERMS, SLOTS, WIDTH, 2 * WIDTH, dtype=BF16)
    flops = 2 * 2 * 32 * 128 * 256 * 256

    start_mine = gather(jnp.broadcast_to(psi[None], (SECS,) + psi.shape))
    start_other = lax.ppermute(start_mine, AXES, OTHER_CORE)
    base, bases, size_of, masks, lefts, rights = call(
        prepare,
        (
            shape(SLOTS, LOCAL_TERMS, dtype=ints),
            chunk,
            shape(SECTORS, dtype=ints),
            vec,
            env_shape,
            env_shape,
        ),
        (SMEM, VMEM, SMEM, VMEM, VMEM, VMEM),
        (HBM,) * 3 + (VMEM,) * 2,
        scratch=(
            pltpu.SMEM((SLOTS, LOCAL_TERMS), ints),
            pltpu.SMEM((SECTORS,), ints),
            pltpu.SMEM((SECTORS,), ints),
            pltpu.SMEM((SECTORS,), ints),
            pltpu.SemaphoreType.DMA((3,)),
        ),
        flops=flops,
        moved=8 << 20,
    )(coupling, assign, sizes, left_env, right_env)
    parts = call(apply_first, parts_shape, VMEM, (SMEM,) + (VMEM,) * 5, flops=flops)(
        base, bases, start_mine, start_other, lefts, rights
    )
    parts = exchange(parts, SAME_SEC)
    sigma_first, copies, other_base = call(
        finish_first,
        (vec, shape(SECS, SLOTS, ROWS, WIDTH), shape(SLOTS, LOCAL_TERMS, dtype=ints)),
        (VMEM,) * 3,
        (VMEM, VMEM),
    )(masks, parts)
    mine = gather(copies)
    packed = call(pack, shape(SLOTS, LOCAL_TERMS, OPS // 2, ROWS, WIDTH), VMEM, (SMEM, VMEM))(
        other_base, mine
    )
    other = lax.ppermute(packed, AXES, OTHER_CORE)
    sums = call(
        moments,
        chunk,
        VMEM,
        (SMEM, VMEM, VMEM),
        scratch=(pltpu.VMEM((SECTORS, ROWS, WIDTH), F32),),
        flops=flops,
    )(size_of, start_mine, mine)
    own = call(
        own_products, shape(SLOTS, LOCAL_TERMS, WIDTH, WIDTH), VMEM, (SMEM, VMEM, VMEM), flops=flops // 2
    )(base, mine, lefts)
    parts = call(apply_next, parts_shape, VMEM, (VMEM,) * 5, flops=flops)(own, other, lefts, rights, sums)
    parts = exchange(parts, SAME_SEC)
    next_vector, sigma_next = call(finish_next, (vec, vec), (VMEM, VMEM), (VMEM,) * 4)(
        masks, parts, psi, sigma_first
    )
    return sigma_first, next_vector, sigma_next


def solution(mesh):
    placed = (
        P("sec", "op", None),
        P("op", "sec", None, None),
        P("op", "sec", None, None),
        P("sec", "op"),
        P(),
        P(),
    )
    return jax.shard_map(
        on_device,
        mesh=mesh,
        in_specs=placed,
        out_specs=(P("sec", "op", None),) * 3,
        check_vma=False,
    )
```

```python
import itertools

import jax
import jax.numpy as jnp
from jax import lax
from jax.experimental import pallas as pl
from jax.experimental.pallas import tpu as pltpu
from jax.sharding import PartitionSpec as P

AXES = ("op", "sec")
F32 = jnp.float32
BF16 = jnp.bfloat16
SLOTS, ROWS, WIDTH, LOCAL_TERMS = 2, 8, 128, 16
SECTORS = 64
OPS, SECS = 16, 32
CHUNKS = 512


PLACES = list(itertools.product(range(4), range(2), range(2), range(8), range(4)))


def number(x, zl, core, y, zh):
    return ((((x * 2 + zl) * 2 + core) * 8) + y) * 4 + zh


def groups(key, order):
    found = {}
    for place in PLACES:
        found.setdefault(key(*place), []).append((order(*place), number(*place)))
    return [[device for _, device in sorted(members)] for members in found.values()]


def cube(x, zl, core, y, zh):
    z = 2 * zh + zl
    return (x + core - 1) % 4 // 2, (y - core) % 8 // 2, (z - core) % 8 // 2, core


def kind(x, zl, core, y, zh):
    return (x + 2 * zl) % 4 * 2 + (y + zl) % 2


SAME_SEC = groups(lambda x, zl, core, y, zh: (y, zh), lambda x, zl, core, y, zh: (x, zl, core))
FAR = groups(lambda *place: (kind(*place), place[2]), lambda x, zl, core, y, zh: (zh, zl, y // 2))
NEAR = groups(cube, kind)
OTHER_CORE = [
    (number(x, zl, core, y, zh), number(x, zl, 1 - core, y, zh)) for x, zl, core, y, zh in PLACES
]


def exchange(parts, members):
    return lax.all_to_all(parts, AXES, 0, 0, axis_index_groups=members)


VMEM = pl.BlockSpec(memory_space=pltpu.VMEM)
SMEM = pl.BlockSpec(memory_space=pltpu.SMEM)
HBM = pl.BlockSpec(memory_space=pltpu.HBM)


def call(body, outs, out_specs, in_specs, scratch=(), flops=0, moved=1 << 20):
    return pl.pallas_call(
        body,
        out_shape=outs,
        in_specs=in_specs,
        out_specs=out_specs,
        scratch_shapes=list(scratch),
        compiler_params=pltpu.CompilerParams(vmem_limit_bytes=40 << 20),
        cost_estimate=pl.CostEstimate(flops=flops, bytes_accessed=moved, transcendentals=0),
    )


def shape(*dims, dtype=F32):
    return jax.ShapeDtypeStruct(dims, dtype)


def inside(size, first_row):
    rows = first_row + lax.broadcasted_iota(jnp.int32, (ROWS, WIDTH), 0)
    cols = lax.broadcasted_iota(jnp.int32, (ROWS, WIDTH), 1)
    return (rows < size) & (cols < size)


def fetch(pairs, done):
    copies = [pltpu.make_async_copy(source, target, done.at[i]) for i, (source, target) in enumerate(pairs)]
    for copy in copies:
        copy.start()
    for copy in copies:
        copy.wait()


def halves(values):
    high = values.astype(BF16)
    return high, (values - high.astype(F32)).astype(BF16)


def prepare(
    coupling_hbm, assign_hbm, sizes_hbm, left, right, bases, size_of, masks, lefts, rights, coupling, assign, sizes, slot_of, done
):
    fetch([(coupling_hbm, coupling), (assign_hbm, assign), (sizes_hbm, sizes)], done)
    op = lax.axis_index("op")
    sub = lax.broadcasted_iota(jnp.int32, (ROWS, WIDTH), 0)
    lane = lax.broadcasted_iota(jnp.int32, (ROWS, WIDTH), 1)
    table = jnp.zeros((ROWS, WIDTH), jnp.int32)
    for p in range(SECTORS):
        sector = assign[p]
        slot_of[sector] = p
        size_of[p] = sizes[sector]
    for t in range(SLOTS):
        for k in range(LOCAL_TERMS):
            p = slot_of[coupling[t, k]]
            y = p // 8
            first = y % 2 * 64 + p % 8 // 2 * 16 + y // 2 * 2 + p % 2
            table = jnp.where((sub == t) & (lane == k), first, table)
        masks[t] = inside(size_of[lax.axis_index("sec") * SLOTS + t], op * ROWS).astype(F32)
    bases[...] = table.astype(F32)
    row = lax.broadcasted_iota(jnp.int32, (WIDTH, WIDTH), 0)
    col = lax.broadcasted_iota(jnp.int32, (WIDTH, WIDTH), 1)
    other = (row // 8 % 2 != op % 2).astype(jnp.int32)
    spot = other * 128 + row // 16 * 8 + row % 8
    lanes = lax.broadcasted_iota(jnp.int32, (WIDTH, 2 * WIDTH), 1)
    spots = jnp.concatenate([spot, spot], axis=1)
    order = jnp.concatenate([lanes == spots, lanes == spots + 64], axis=0).astype(F32).astype(BF16)
    for k in range(LOCAL_TERMS):
        for t in range(SLOTS):
            size = sizes[coupling[t, k]]
            high, low = halves(jnp.where(col < size, left[k, t], 0.0))
            lefts[k, t] = matmul(jnp.concatenate([high, low], axis=1), order).astype(BF16)
            high, low = halves(jnp.where(col < size, right[k, t], 0.0).T)
            rights[k, t, :, :WIDTH] = high
            rights[k, t, :, WIDTH:] = low


def matmul(a, b):
    return lax.dot_general(a, b, (((1,), (0,)), ((), ())), preferred_element_type=F32)


def part_product(columns, chunks):
    high, low = halves(jnp.concatenate(chunks, axis=0))
    pair = jnp.concatenate([high, low], axis=1)
    result = matmul(columns, jnp.concatenate([pair, pair], axis=0))
    return result[:, :WIDTH] + result[:, WIDTH:]


def own_products(bases, mine, lefts, inner):
    base = bases[...].astype(jnp.int32)
    for t in range(SLOTS):
        for k in range(LOCAL_TERMS):
            inner[t, k] = part_product(lefts[k, t, :, :WIDTH], own_rows(mine, base[t, k]))


def products(other_rows, inner, lefts, rights, out):
    for t in range(SLOTS):
        total = jnp.zeros((WIDTH, 2 * WIDTH), F32)
        for k in range(LOCAL_TERMS):
            high, low = halves(inner[t, k] + part_product(lefts[k, t, :, WIDTH:], other_rows(t, k)))
            rows = rights[k, t]
            total = total + matmul(
                jnp.concatenate([high, low], axis=1), jnp.concatenate([rows, rows], axis=0)
            )
        result = total[:, :WIDTH] + total[:, WIDTH:]
        for i in range(OPS):
            out[i, t] = result[i * ROWS : (i + 1) * ROWS]


def own_rows(field, first):
    starts = (first, first ^ 64)
    return [field[starts[zl] + ((x + 2 * zl) % 4 * 128 + zl * 8)] for x in range(4) for zl in range(2)]


def apply_first(bases, inner, other, lefts, rights, out):
    base = bases[...].astype(jnp.int32)
    products(lambda t, k: own_rows(other, base[t, k]), inner, lefts, rights, out)
    for i in range(OPS):
        out[i, SLOTS] = bases[...]


def reduced(parts, t):
    total = parts[0, t]
    for i in range(1, OPS):
        total = total + parts[i, t]
    return total


def finish_first(masks, parts, sigma, copies, other_base):
    op = lax.axis_index("op")
    for t in range(SLOTS):
        total = reduced(parts, t) * masks[t]
        sigma[t] = total
        for i in range(SECS):
            copies[i, t] = total
    numbers = parts[op + 1 - 2 * (op % 2), SLOTS]
    other_base[...] = numbers[:SLOTS, :LOCAL_TERMS].astype(jnp.int32)


def pack(other_base, mine, packed):
    base = other_base[...]
    for t in range(SLOTS):
        for k in range(LOCAL_TERMS):
            for n, chunk in enumerate(own_rows(mine, base[t, k])):
                packed[t, k, n] = chunk


LANES = 4


def whole_sum(values):
    return jnp.sum(jnp.sum(values, axis=1, keepdims=True), axis=0, keepdims=True)


def scan(step, count):
    x, zl = lax.axis_index("op") // 4, lax.axis_index("op") // 2 % 2
    start = (x + 2 * zl) % 4 * 128 + zl * 8
    sums = [jnp.zeros((ROWS, WIDTH), F32)] * (count * LANES)
    for u, (yl, zh, yh, t) in enumerate(itertools.product(range(2), range(4), range(4), range(2))):
        for n, term in enumerate(step(u, (yl, zh, yh, t), start + (yl * 64 + zh * 16 + yh * 2 + t))):
            at = n * LANES + u % LANES
            sums[at] = sums[at] + term
    return [whole_sum(sum(sums[n : n + LANES])) for n in range(0, len(sums), LANES)]


def projection(cross, square):
    some = square > 0.0
    return jnp.where(some, cross / jnp.where(some, square, 1.0), 0.0)


def moments(size_of, start, field, sums, masked):
    op = lax.axis_index("op")
    rows = lax.broadcasted_iota(jnp.int32, (ROWS, WIDTH), 0)
    cols = lax.broadcasted_iota(jnp.int32, (ROWS, WIDTH), 1)

    def first(u, where, here):
        yl, zh, yh, t = where
        y = yh * 2 + (yl + op // 2) % 2
        size = size_of[y * 8 + zh * 2 + t]
        s = jnp.where((cols < size) & (rows < size - op * ROWS), start[here], 0.0)
        masked[u] = s
        return s * field[here], s * s

    cross, square = scan(first, 2)
    theta = projection(cross, square)

    def second(u, where, here):
        r = field[here] - theta * masked[u]
        return (r * r,)

    (left,) = scan(second, 1)
    sums[...] = jnp.where(rows == 0, cross, jnp.where(rows == 1, square, left))


def apply_next(inner, packed, lefts, rights, sums, out):
    products(lambda t, k: [packed[t, k, n] for n in range(OPS // 2)], inner, lefts, rights, out)
    for i in range(OPS):
        out[i, SLOTS] = sums[...]


def finish_next(masks, parts, psi, sigma, next_vector, sigma_next):
    cross, square, left = [
        jnp.concatenate([parts[i, SLOTS, n : n + 1] for i in range(OPS)], axis=0) for n in range(3)
    ]
    theta = jnp.sum(cross, axis=0, keepdims=True) / jnp.sum(square, axis=0, keepdims=True)
    shift = projection(cross, square) - theta
    norm = jnp.sum(left + shift * square * shift, axis=0, keepdims=True)
    scale = 1.0 / jnp.sqrt(norm + 1e-06)
    for t in range(SLOTS):
        sigma_next[t] = (reduced(parts, t) * masks[t] - theta * sigma[t]) * scale
        next_vector[t] = (sigma[t] - theta * (psi[t] * masks[t])) * scale


def gather(copies):
    part = exchange(copies, FAR).reshape(1, CHUNKS // 8, ROWS, WIDTH)
    part = jnp.broadcast_to(part, (8, CHUNKS // 8, ROWS, WIDTH))
    return exchange(part, NEAR).reshape(CHUNKS, ROWS, WIDTH)


def on_device(psi, left_env, right_env, coupling, assign, sizes):
    ints = jnp.int32
    vec = shape(SLOTS, ROWS, WIDTH)
    chunk = shape(ROWS, WIDTH)
    parts_shape = shape(OPS, SLOTS + 1, ROWS, WIDTH)
    env_shape = shape(LOCAL_TERMS, SLOTS, WIDTH, 2 * WIDTH, dtype=BF16)
    flops = 2 * 2 * 32 * 128 * 256 * 256

    start_mine = gather(jnp.broadcast_to(psi[None], (SECS,) + psi.shape))
    start_other = lax.ppermute(start_mine, AXES, OTHER_CORE)
    bases, size_of, masks, lefts, rights = call(
        prepare,
        (
            chunk,
            shape(SECTORS, dtype=ints),
            vec,
            env_shape,
            env_shape,
        ),
        (VMEM, SMEM, VMEM, VMEM, VMEM),
        (HBM,) * 3 + (VMEM,) * 2,
        scratch=(
            pltpu.SMEM((SLOTS, LOCAL_TERMS), ints),
            pltpu.SMEM((SECTORS,), ints),
            pltpu.SMEM((SECTORS,), ints),
            pltpu.SMEM((SECTORS,), ints),
            pltpu.SemaphoreType.DMA((3,)),
        ),
        flops=flops,
        moved=8 << 20,
    )(coupling, assign, sizes, left_env, right_env)
    inner_shape = shape(SLOTS, LOCAL_TERMS, WIDTH, WIDTH)
    own = call(own_products, inner_shape, VMEM, (VMEM,) * 3, flops=flops // 2)
    parts = call(apply_first, parts_shape, VMEM, (VMEM,) * 5, flops=flops)(
        bases, own(bases, start_mine, lefts), start_other, lefts, rights
    )
    parts = exchange(parts, SAME_SEC)
    sigma_first, copies, other_base = call(
        finish_first,
        (vec, shape(SECS, SLOTS, ROWS, WIDTH), shape(SLOTS, LOCAL_TERMS, dtype=ints)),
        (VMEM,) * 3,
        (VMEM, VMEM),
    )(masks, parts)
    mine = gather(copies)
    packed = call(pack, shape(SLOTS, LOCAL_TERMS, OPS // 2, ROWS, WIDTH), VMEM, (VMEM, VMEM))(
        other_base, mine
    )
    other = lax.ppermute(packed, AXES, OTHER_CORE)
    sums = call(
        moments,
        chunk,
        VMEM,
        (SMEM, VMEM, VMEM),
        scratch=(pltpu.VMEM((SECTORS, ROWS, WIDTH), F32),),
        flops=flops,
    )(size_of, start_mine, mine)
    parts = call(apply_next, parts_shape, VMEM, (VMEM,) * 5, flops=flops)(
        own(bases, mine, lefts), other, lefts, rights, sums
    )
    parts = exchange(parts, SAME_SEC)
    next_vector, sigma_next = call(finish_next, (vec, vec), (VMEM, VMEM), (VMEM,) * 4)(
        masks, parts, psi, sigma_first
    )
    return sigma_first, next_vector, sigma_next


def solution(mesh):
    placed = (
        P("sec", "op", None),
        P("op", "sec", None, None),
        P("op", "sec", None, None),
        P("sec", "op"),
        P(),
        P(),
    )
    return jax.shard_map(
        on_device,
        mesh=mesh,
        in_specs=placed,
        out_specs=(P("sec", "op", None),) * 3,
        check_vma=False,
    )
```

```python
import itertools

import jax
import jax.numpy as jnp
from jax import lax
from jax.experimental import pallas as pl
from jax.experimental.pallas import tpu as pltpu
from jax.sharding import PartitionSpec as P

AXES = ("op", "sec")
F32 = jnp.float32
BF16 = jnp.bfloat16
SLOTS, ROWS, WIDTH, LOCAL_TERMS = 2, 8, 128, 16
SECTORS = 64
OPS, SECS = 16, 32
CHUNKS = 512


PLACES = list(itertools.product(range(4), range(2), range(2), range(8), range(4)))


def number(x, zl, core, y, zh):
    return ((((x * 2 + zl) * 2 + core) * 8) + y) * 4 + zh


def groups(key, order):
    found = {}
    for place in PLACES:
        found.setdefault(key(*place), []).append((order(*place), number(*place)))
    return [[device for _, device in sorted(members)] for members in found.values()]


def cube(x, zl, core, y, zh):
    z = 2 * zh + zl
    return (x - core) % 4 // 2, (y - core) % 8 // 2, (z - core) % 8 // 2, core


def kind(x, zl, core, y, zh):
    return (x + 2 * zl) % 4 * 2 + (y + zl) % 2


SAME_SEC = groups(lambda x, zl, core, y, zh: (y, zh), lambda x, zl, core, y, zh: (x, zl, core))
FAR = groups(lambda *place: (kind(*place), place[2]), lambda x, zl, core, y, zh: (zh, zl, y // 2))
NEAR = groups(cube, kind)
OTHER_CORE = [
    (number(x, zl, core, y, zh), number(x, zl, 1 - core, y, zh)) for x, zl, core, y, zh in PLACES
]


def exchange(parts, members):
    return lax.all_to_all(parts, AXES, 0, 0, axis_index_groups=members)


VMEM = pl.BlockSpec(memory_space=pltpu.VMEM)
SMEM = pl.BlockSpec(memory_space=pltpu.SMEM)
HBM = pl.BlockSpec(memory_space=pltpu.HBM)


def call(body, outs, out_specs, in_specs, scratch=(), flops=0, moved=1 << 20):
    return pl.pallas_call(
        body,
        out_shape=outs,
        in_specs=in_specs,
        out_specs=out_specs,
        scratch_shapes=list(scratch),
        compiler_params=pltpu.CompilerParams(vmem_limit_bytes=40 << 20),
        cost_estimate=pl.CostEstimate(flops=flops, bytes_accessed=moved, transcendentals=0),
    )


def shape(*dims, dtype=F32):
    return jax.ShapeDtypeStruct(dims, dtype)


def inside(size, first_row):
    rows = first_row + lax.broadcasted_iota(jnp.int32, (ROWS, WIDTH), 0)
    cols = lax.broadcasted_iota(jnp.int32, (ROWS, WIDTH), 1)
    return (rows < size) & (cols < size)


def fetch(pairs, done):
    copies = [pltpu.make_async_copy(source, target, done.at[i]) for i, (source, target) in enumerate(pairs)]
    for copy in copies:
        copy.start()
    for copy in copies:
        copy.wait()


def halves(values):
    high = values.astype(BF16)
    return high, (values - high.astype(F32)).astype(BF16)


def prepare(
    coupling_hbm, assign_hbm, sizes_hbm, left, right, bases, size_of, masks, lefts, rights, coupling, assign, sizes, slot_of, done
):
    fetch([(coupling_hbm, coupling), (assign_hbm, assign), (sizes_hbm, sizes)], done)
    op = lax.axis_index("op")
    sub = lax.broadcasted_iota(jnp.int32, (ROWS, WIDTH), 0)
    lane = lax.broadcasted_iota(jnp.int32, (ROWS, WIDTH), 1)
    table = jnp.zeros((ROWS, WIDTH), jnp.int32)
    for p in range(SECTORS):
        sector = assign[p]
        slot_of[sector] = p
        size_of[p] = sizes[sector]
    for t in range(SLOTS):
        for k in range(LOCAL_TERMS):
            p = slot_of[coupling[t, k]]
            y = p // 8
            first = y % 2 * 64 + p % 8 // 2 * 16 + y // 2 * 2 + p % 2
            table = jnp.where((sub == t) & (lane == k), first, table)
        masks[t] = inside(size_of[lax.axis_index("sec") * SLOTS + t], op * ROWS).astype(F32)
    bases[...] = table.astype(F32)
    row = lax.broadcasted_iota(jnp.int32, (WIDTH, WIDTH), 0)
    col = lax.broadcasted_iota(jnp.int32, (WIDTH, WIDTH), 1)
    other = (row // 8 % 2 != op % 2).astype(jnp.int32)
    spot = other * 128 + row // 16 * 8 + row % 8
    lanes = lax.broadcasted_iota(jnp.int32, (WIDTH, 2 * WIDTH), 1)
    spots = jnp.concatenate([spot, spot], axis=1)
    order = jnp.concatenate([lanes == spots, lanes == spots + 64], axis=0).astype(F32).astype(BF16)
    for k in range(LOCAL_TERMS):
        for t in range(SLOTS):
            size = sizes[coupling[t, k]]
            high, low = halves(jnp.where(col < size, left[k, t], 0.0))
            lefts[k, t] = matmul(jnp.concatenate([high, low], axis=1), order).astype(BF16)
            high, low = halves(jnp.where(col < size, right[k, t], 0.0).T)
            rights[k, t, :, :WIDTH] = high
            rights[k, t, :, WIDTH:] = low


def matmul(a, b):
    return lax.dot_general(a, b, (((1,), (0,)), ((), ())), preferred_element_type=F32)


def part_product(columns, chunks):
    high, low = halves(jnp.concatenate(chunks, axis=0))
    pair = jnp.concatenate([high, low], axis=1)
    result = matmul(columns, jnp.concatenate([pair, pair], axis=0))
    return result[:, :WIDTH] + result[:, WIDTH:]


def own_products(bases, mine, lefts, inner):
    base = bases[...].astype(jnp.int32)
    for t in range(SLOTS):
        for k in range(LOCAL_TERMS):
            inner[t, k] = part_product(lefts[k, t, :, :WIDTH], own_rows(mine, base[t, k]))


def products(other_rows, inner, lefts, rights, out):
    for t in range(SLOTS):
        total = jnp.zeros((WIDTH, 2 * WIDTH), F32)
        for k in range(LOCAL_TERMS):
            high, low = halves(inner[t, k] + part_product(lefts[k, t, :, WIDTH:], other_rows(t, k)))
            rows = rights[k, t]
            total = total + matmul(
                jnp.concatenate([high, low], axis=1), jnp.concatenate([rows, rows], axis=0)
            )
        result = total[:, :WIDTH] + total[:, WIDTH:]
        for i in range(OPS):
            out[i, t] = result[i * ROWS : (i + 1) * ROWS]


def own_rows(field, first):
    starts = (first, first ^ 64)
    return [field[starts[zl] + ((x + 2 * zl) % 4 * 128 + zl * 8)] for x in range(4) for zl in range(2)]


def apply_first(bases, inner, other, lefts, rights, out):
    base = bases[...].astype(jnp.int32)
    products(lambda t, k: own_rows(other, base[t, k]), inner, lefts, rights, out)
    for i in range(OPS):
        out[i, SLOTS] = bases[...]


def reduced(parts, t):
    total = parts[0, t]
    for i in range(1, OPS):
        total = total + parts[i, t]
    return total


def finish_first(masks, parts, sigma, copies, other_base):
    op = lax.axis_index("op")
    for t in range(SLOTS):
        total = reduced(parts, t) * masks[t]
        sigma[t] = total
        for i in range(SECS):
            copies[i, t] = total
    numbers = parts[op + 1 - 2 * (op % 2), SLOTS]
    other_base[...] = numbers[:SLOTS, :LOCAL_TERMS].astype(jnp.int32)


def pack(other_base, mine, packed):
    base = other_base[...]
    for t in range(SLOTS):
        for k in range(LOCAL_TERMS):
            for n, chunk in enumerate(own_rows(mine, base[t, k])):
                packed[t, k, n] = chunk


LANES = 4


def whole_sum(values):
    return jnp.sum(jnp.sum(values, axis=1, keepdims=True), axis=0, keepdims=True)


def scan(step, count):
    x, zl = lax.axis_index("op") // 4, lax.axis_index("op") // 2 % 2
    start = (x + 2 * zl) % 4 * 128 + zl * 8
    sums = [jnp.zeros((ROWS, WIDTH), F32)] * (count * LANES)
    for u, (yl, zh, yh, t) in enumerate(itertools.product(range(2), range(4), range(4), range(2))):
        for n, term in enumerate(step(u, (yl, zh, yh, t), start + (yl * 64 + zh * 16 + yh * 2 + t))):
            at = n * LANES + u % LANES
            sums[at] = sums[at] + term
    return [whole_sum(sum(sums[n : n + LANES])) for n in range(0, len(sums), LANES)]


def projection(cross, square):
    some = square > 0.0
    return jnp.where(some, cross / jnp.where(some, square, 1.0), 0.0)


def moments(size_of, start, field, sums, masked):
    op = lax.axis_index("op")
    rows = lax.broadcasted_iota(jnp.int32, (ROWS, WIDTH), 0)
    cols = lax.broadcasted_iota(jnp.int32, (ROWS, WIDTH), 1)

    def first(u, where, here):
        yl, zh, yh, t = where
        y = yh * 2 + (yl + op // 2) % 2
        size = size_of[y * 8 + zh * 2 + t]
        s = jnp.where((cols < size) & (rows < size - op * ROWS), start[here], 0.0)
        masked[u] = s
        return s * field[here], s * s

    cross, square = scan(first, 2)
    theta = projection(cross, square)

    def second(u, where, here):
        r = field[here] - theta * masked[u]
        return (r * r,)

    (left,) = scan(second, 1)
    sums[...] = jnp.where(rows == 0, cross, jnp.where(rows == 1, square, left))


def apply_next(inner, packed, lefts, rights, sums, out):
    products(lambda t, k: [packed[t, k, n] for n in range(OPS // 2)], inner, lefts, rights, out)
    for i in range(OPS):
        out[i, SLOTS] = sums[...]


def finish_next(masks, parts, psi, sigma, next_vector, sigma_next):
    cross, square, left = [
        jnp.concatenate([parts[i, SLOTS, n : n + 1] for i in range(OPS)], axis=0) for n in range(3)
    ]
    theta = jnp.sum(cross, axis=0, keepdims=True) / jnp.sum(square, axis=0, keepdims=True)
    shift = projection(cross, square) - theta
    norm = jnp.sum(left + shift * square * shift, axis=0, keepdims=True)
    scale = 1.0 / jnp.sqrt(norm + 1e-06)
    for t in range(SLOTS):
        sigma_next[t] = (reduced(parts, t) * masks[t] - theta * sigma[t]) * scale
        next_vector[t] = (sigma[t] - theta * (psi[t] * masks[t])) * scale


def gather(copies):
    part = exchange(copies, FAR).reshape(1, CHUNKS // 8, ROWS, WIDTH)
    part = jnp.broadcast_to(part, (8, CHUNKS // 8, ROWS, WIDTH))
    return exchange(part, NEAR).reshape(CHUNKS, ROWS, WIDTH)


def on_device(psi, left_env, right_env, coupling, assign, sizes):
    ints = jnp.int32
    vec = shape(SLOTS, ROWS, WIDTH)
    chunk = shape(ROWS, WIDTH)
    parts_shape = shape(OPS, SLOTS + 1, ROWS, WIDTH)
    env_shape = shape(LOCAL_TERMS, SLOTS, WIDTH, 2 * WIDTH, dtype=BF16)
    flops = 2 * 2 * 32 * 128 * 256 * 256

    start_mine = gather(jnp.broadcast_to(psi[None], (SECS,) + psi.shape))
    start_other = lax.ppermute(start_mine, AXES, OTHER_CORE)
    bases, size_of, masks, lefts, rights = call(
        prepare,
        (
            chunk,
            shape(SECTORS, dtype=ints),
            vec,
            env_shape,
            env_shape,
        ),
        (VMEM, SMEM, VMEM, VMEM, VMEM),
        (HBM,) * 3 + (VMEM,) * 2,
        scratch=(
            pltpu.SMEM((SLOTS, LOCAL_TERMS), ints),
            pltpu.SMEM((SECTORS,), ints),
            pltpu.SMEM((SECTORS,), ints),
            pltpu.SMEM((SECTORS,), ints),
            pltpu.SemaphoreType.DMA((3,)),
        ),
        flops=flops,
        moved=8 << 20,
    )(coupling, assign, sizes, left_env, right_env)
    inner_shape = shape(SLOTS, LOCAL_TERMS, WIDTH, WIDTH)
    own = call(own_products, inner_shape, VMEM, (VMEM,) * 3, flops=flops // 2)
    parts = call(apply_first, parts_shape, VMEM, (VMEM,) * 5, flops=flops)(
        bases, own(bases, start_mine, lefts), start_other, lefts, rights
    )
    parts = exchange(parts, SAME_SEC)
    sigma_first, copies, other_base = call(
        finish_first,
        (vec, shape(SECS, SLOTS, ROWS, WIDTH), shape(SLOTS, LOCAL_TERMS, dtype=ints)),
        (VMEM,) * 3,
        (VMEM, VMEM),
    )(masks, parts)
    mine = gather(copies)
    packed = call(pack, shape(SLOTS, LOCAL_TERMS, OPS // 2, ROWS, WIDTH), VMEM, (VMEM, VMEM))(
        other_base, mine
    )
    other = lax.ppermute(packed, AXES, OTHER_CORE)
    sums = call(
        moments,
        chunk,
        VMEM,
        (SMEM, VMEM, VMEM),
        scratch=(pltpu.VMEM((SECTORS, ROWS, WIDTH), F32),),
        flops=flops,
    )(size_of, start_mine, mine)
    parts = call(apply_next, parts_shape, VMEM, (VMEM,) * 5, flops=flops)(
        own(bases, mine, lefts), other, lefts, rights, sums
    )
    parts = exchange(parts, SAME_SEC)
    next_vector, sigma_next = call(finish_next, (vec, vec), (VMEM, VMEM), (VMEM,) * 4)(
        masks, parts, psi, sigma_first
    )
    return sigma_first, next_vector, sigma_next


def solution(mesh):
    placed = (
        P("sec", "op", None),
        P("op", "sec", None, None),
        P("op", "sec", None, None),
        P("sec", "op"),
        P(),
        P(),
    )
    return jax.shard_map(
        on_device,
        mesh=mesh,
        in_specs=placed,
        out_specs=(P("sec", "op", None),) * 3,
        check_vma=False,
    )
```
